256 devices in a mesh: samp: 8 (over x, z_lo), par: 32 (over y, z_hi, core).
Axes of the slice: x: 4, y: 4, z: 8 (z_hi: 4, z_lo: 2; z = z_hi * 2 + z_lo), core: 2. Of those that a mesh axis runs over, the one named last changes fastest.
Arguments:
- log_derivs: float32 [4096, 32768], P('samp', 'par')
- spins: int32 [4096, 100], P('samp'), may hold values from 0 to 1
- roster: int32 [2, 512], replicated, may hold values from 0 to 4095, as said below
Outputs:
- gram_tiles: float32 [8, 3, 512, 512], P('samp', None, 'par')
The draws below stay inside these ranges and needn't reach their ends.
Inputs may be any that keep to these rules, and one draw needn't show every extreme that they name: In each round r all entries share one quotient m_r = roster[r, j] // 512; the m_r of different rounds are distinct and one of them is 7; the remainders roster[r, j] % 512 of a round are a permutation of 0 to 511.
All inputs are finite; a program needn't handle non-finite values.
Results may differ from the reference program's by a relative error of at most 0.0003.
Values sent between devices are 32-bit elements; how exact they have to be, the bound alone decides.
A program may use at most 64 MiB of HBM per device.

```python
import math
import jax
import jax.numpy as jnp
from jax import lax

SG = 512
LSIDE = 10
NSITES = 100
NGROUPS = 8
ROUNDS = 2
SAMPLES = 4096
PARAMS = 32768


def draw_log_derivs(key, part):
    key = jax.random.fold_in(key, 7)
    key_rows, key_cols, key_common, key_shape, key_noise = jax.random.split(key, 5)
    row_scale = jnp.exp(jax.random.uniform(key_rows, (SAMPLES, 1), jnp.float32) * math.log(10.0))
    col_scale = jnp.exp(jax.random.uniform(key_cols, (1, PARAMS), jnp.float32) * math.log(10.0))
    common = jax.random.normal(key_common, (SAMPLES, 1), jnp.float32)
    shape_col = jax.random.normal(key_shape, (1, PARAMS), jnp.float32)
    noise = jax.random.normal(key_noise, (SAMPLES, PARAMS), jnp.float32)
    factor = 0.1 * math.sqrt(SAMPLES / PARAMS)
    return (factor * row_scale * (noise * col_scale + 3.0 * common * shape_col)).astype(jnp.float32)


def draw_roster(key, part):
    key = jax.random.fold_in(key, 11)
    key_other, key_order, key_perm = jax.random.split(key, 3)
    other_mask = jax.random.randint(key_other, (), 0, NGROUPS - 1, jnp.int32)
    order_bit = jax.random.randint(key_order, (), 0, 2, jnp.int32)
    first_mask = jnp.where(order_bit == 1, other_mask, NGROUPS - 1)
    second_mask = jnp.where(order_bit == 1, NGROUPS - 1, other_mask)
    masks = jnp.stack([first_mask, second_mask])[:ROUNDS].astype(jnp.int32)
    perm_keys = jax.random.split(key_perm, ROUNDS)
    orders = jnp.stack([jax.random.permutation(perm_keys[index], SG).astype(jnp.int32) for index in range(ROUNDS)])
    return (masks[:, None] * SG + orders).astype(jnp.int32)


def set_ends(array, own_key, low, top_value):
    dims = array.shape
    index_at = [jax.random.randint(jax.random.fold_in(own_key, axis), (), 0, dims[axis]) for axis in range(len(dims))]
    array = array.at[tuple(index_at)].set(low)
    longest = dims.index(max(dims))
    index_at[longest] = (index_at[longest] + 1) % dims[longest]
    return array.at[tuple(index_at)].set(top_value)


def setup_inputs(seed: int = 0) -> dict:
    seeds = jax.random.split(jax.random.key(seed), 4)
    log_derivs = draw_log_derivs(jax.random.fold_in(seeds[3], 71), 0)
    spins = set_ends(jax.random.randint(seeds[1], (SAMPLES, NSITES), 0, 2), jax.random.fold_in(seeds[1], 1), 0, 1).astype(jnp.int32)
    roster = draw_roster(jax.random.fold_in(seeds[3], 71), 0)
    return dict(log_derivs=log_derivs, spins=spins, roster=roster)


def marshall_signs(spins):
    site_index = jnp.arange(NSITES, dtype=jnp.int32)
    sublattice = (((site_index // LSIDE) + (site_index % LSIDE)) % 2 == 0).astype(jnp.int32)
    parity = jnp.sum(spins * sublattice[None, :], axis=1) % 2
    return (1 - 2 * parity).astype(jnp.float32)


def gram_block(left_rows, right_rows):
    return lax.dot_general(left_rows, right_rows, (((1,), (1,)), ((), ())), precision=lax.Precision.HIGHEST, preferred_element_type=jnp.float32)


def reference(log_derivs, spins, roster):
    marshall = marshall_signs(spins)
    signed = log_derivs * marshall[:, None]
    column_mean = jnp.sum(signed, axis=0) / SAMPLES
    centered = signed - column_mean[None, :]

    def one_group(group):
        own_rows = lax.dynamic_slice_in_dim(centered, (group * SG).astype(jnp.int32), SG, 0)
        gram_tiles = [gram_block(own_rows, own_rows) / SAMPLES]
        for round_index in range(ROUNDS):
            entries = roster[round_index]
            partner = jnp.bitwise_xor(group, entries // SG).astype(jnp.int32)
            picked = (partner * SG + entries % SG).astype(jnp.int32)
            other_rows = jnp.take(centered, picked, axis=0)
            gram_tiles.append(gram_block(own_rows, other_rows) / SAMPLES)
        return jnp.stack(gram_tiles)

    return lax.map(one_group, jnp.arange(NGROUPS, dtype=jnp.int32))
```

```python
import functools

import jax
import jax.numpy as jnp
from jax import lax
from jax.experimental import pallas as pl
from jax.experimental.pallas import tpu as pltpu
from jax.sharding import PartitionSpec as P

MESH = pl.DeviceIdType.MESH
F32, BF16 = jnp.float32, jnp.bfloat16

SG = 512
NSITES = 100
LSIDE = 10
COLS = 1024
HALF = COLS // 2
SAMPLES = 4096
SUBS = 8
PARTS = 4

ROUTES = {
    0: [("own", 1, "T"), ("T", 6, "B7")],
    1: [("own", 1, "Bm"), ("Bm", 6, "B7")],
    2: [("own", 6, "T"), ("own", 2, "Bm"), ("T", 1, "B7")],
    3: [("own", 1, "T"), ("T", 6, "B7"), ("T", 2, "Bm")],
    4: [("own", 6, "T"), ("T", 1, "B7"), ("T", 2, "Bm")],
    5: [("own", 6, "T"), ("T", 1, "B7"), ("B7", 2, "Bm")],
    6: [("own", 6, "Bm"), ("Bm", 1, "B7")],
}


def bit_of(value, index):
    return lax.rem(lax.div(value, jnp.int32(2**index)), jnp.int32(2))


def flip(value, mask, bits):
    total = jnp.int32(0)
    for index in range(bits):
        bit = bit_of(value, index)
        total = total + (1 - bit if mask >> index & 1 else bit) * 2**index
    return total


def dot_nt(left, right):
    return lax.dot_general(left, right, (((1,), (1,)), ((), ())), preferred_element_type=F32)


def split(value):
    high = value.astype(BF16)
    return high, (value - high.astype(F32)).astype(BF16)


def product(left, right):
    (left_high, left_low), (right_high, right_low) = left, right
    return dot_nt(left_high, right_high) + (dot_nt(left_high, right_low) + dot_nt(left_low, right_high))


def kernel(m, x_hbm, spins_ref, roster_ref, out_ref, *scratch):
    (rows, buf_t, buf_7, buf_m, sums, mean_ref, c_high, c_low, b_high, b_low, pay_d, pay_c,
     r0_d, r0_c, r1_d, r1_c, r2_d, r2_c, r3_d, r3_c, r4_d, r4_c, cross, picks,
     load_sem, send_sem, recv_sem) = scratch
    kinds = 1 if m == 0 else 2
    group = lax.axis_index("samp")
    part = lax.axis_index("par")
    core = lax.rem(part, jnp.int32(2))
    zh = lax.rem(lax.div(part, jnp.int32(2)), jnp.int32(4))
    y = lax.div(part, jnp.int32(8))
    side_bit = 0 if m == 0 else (m & -m).bit_length() - 1
    side = bit_of(group, side_bit)
    own_half = pl.ds(pl.multiple_of(side * HALF, HALF), HALF)
    sent_half = pl.ds(pl.multiple_of((1 - side) * HALF, HALF), HALF)

    def samp_peer(mask):
        return {"samp": flip(group, mask, 3)}

    def par_peer(new_y, new_zh, new_core):
        return {"par": new_y * 8 + new_zh * 2 + new_core}

    loads = [pltpu.make_async_copy(x_hbm.at[:, c], rows.at[c], load_sem.at[c]) for c in range(2)]
    for load in loads:
        load.start()

    peers = [samp_peer(mask) for mask in range(1, 8)]
    peers += [par_peer(y, zh, 1 - core)]
    peers += [par_peer(flip(y, mask, 2), zh, core) for mask in (1, 3)]
    peers += [par_peer(y, flip(zh, mask, 2), core) for mask in (1, 3)]
    barrier = pltpu.get_barrier_semaphore()
    for peer in peers:
        pl.semaphore_signal(barrier, inc=1, device_id=peer, device_id_type=MESH)

    started = []
    counter = [0]

    def remote(src, dst, peer):
        index = counter[0]
        counter[0] += 1
        return pltpu.make_async_remote_copy(
            src_ref=src, dst_ref=dst, send_sem=send_sem.at[index], recv_sem=recv_sem.at[index],
            device_id=peer, device_id_type=MESH,
        )

    buffers = {"T": buf_t, "B7": buf_7, "Bm": buf_m}
    depth_of = {"own": 0}
    levels = []
    for src, hop, dst in ROUTES[m]:
        depth_of[dst] = depth_of[src] + 1
        copies = []
        for sub in range(SUBS):
            c, first = sub // PARTS, (sub % PARTS) * 8
            at = (c, pl.ds(first, 8))
            src_ref = rows.at[at + (slice(None), sent_half)] if src == "own" else buffers[src].at[at]
            copies.append(remote(src_ref, buffers[dst].at[at], samp_peer(hop)))
        if depth_of[src] == len(levels):
            levels.append([])
        levels[depth_of[src]].append(copies)
    depth = len(levels)

    def exchange(slot):
        for level in range(depth):
            sub = slot - level
            if not 0 <= sub < SUBS:
                continue
            for copies in levels[level]:
                copies[sub].wait_recv()
            if level + 1 < depth:
                for copies in levels[level + 1]:
                    copies[sub].start()
                    started.append(copies[sub])
            if level == 0:
                for copies in levels[0]:
                    copies[sub].wait_send()
                    if sub + 2 < SUBS:
                        copies[sub + 2].start()

    site = lax.broadcasted_iota(jnp.int32, (1, 1, NSITES), 2)
    on_a = (1 - lax.rem(lax.div(site, jnp.int32(LSIDE)) + lax.rem(site, jnp.int32(LSIDE)), jnp.int32(2))).astype(F32)
    pl.semaphore_wait(barrier, len(peers))
    column_sum = jnp.zeros((8, COLS), F32)
    for sub in range(SUBS):
        c, first = sub // PARTS, (sub % PARTS) * 8
        if sub % PARTS == 0:
            loads[c].wait()
        count = jnp.sum(spins_ref[pl.ds(first, 8), c].astype(F32) * on_a, axis=2, keepdims=True)
        sign = 1.0 - 2.0 * (count - 2.0 * jnp.floor(count * 0.5))
        signed = rows[c, pl.ds(first, 8)] * sign
        rows[c, pl.ds(first, 8)] = signed
        column_sum = column_sum + jnp.sum(signed, axis=0)
        if sub < 2:
            for copies in levels[0]:
                copies[sub].start()
    sums[0] = jnp.sum(column_sum, axis=0, keepdims=True)
    sum_copies = [remote(sums.at[0], sums.at[mask], samp_peer(mask)) for mask in range(1, 8)]
    for copy in sum_copies:
        copy.start()
        started.append(copy)

    masks = lax.shift_right_logical(roster_ref[...], 9)
    within = roster_ref[...] & (SG - 1)
    seven_first = masks[0:1] == 7
    natural = lax.broadcasted_iota(jnp.int32, (1, SG), 1)
    plans = [
        natural,
        jnp.where(seven_first, within[0:1], within[1:2]),
        jnp.where(seven_first, within[1:2], within[0:1]),
    ]

    def place_picks():
        for index, plan in enumerate(plans):
            place = ((plan >> 3) & 1) * 256 + (plan >> 4) * 8 + (plan & 7)
            for first in range(0, SG, 128):
                position = lax.broadcasted_iota(jnp.int32, (128, SG), 0) + first
                picks[index, pl.ds(first, 128)] = jnp.where(position == place, 1.0, 0.0).astype(BF16)

    place_picks()

    for copy in sum_copies:
        copy.wait_recv()
    mean_ref[...] = (
        ((sums[0] + sums[1]) + (sums[2] + sums[3])) + ((sums[4] + sums[5]) + (sums[6] + sums[7]))
    ) * (1.0 / SAMPLES)

    for sub in range(SUBS):
        c, first = sub // PARTS, (sub % PARTS) * 8
        at = pl.ds(sub * 64, 64)
        c_high[at], c_low[at] = split(rows[c, pl.ds(first, 8)].reshape(64, COLS) - mean_ref[...])

    def diagonal():
        def block(c, _):
            at = pl.ds(pl.multiple_of(c * 256, 256), 256)
            tile = product((c_high[at], c_low[at]), (c_high[...], c_low[...])).reshape(4, 4, 2, 8, SG)
            for half in range(2):
                pay_d[half, :, :, c] = tile[:, :, half]
            return 0

        lax.fori_loop(0, 2, block, 0)

    def chunk(c):
        pay = pay_c.at[c]
        for kind, buffer in enumerate((buf_7, buf_m)[:kinds]):
            b_high[kind], b_low[kind] = split(buffer[c].reshape(256, HALF) - mean_ref[:, own_half])
            other = b_high[kind], b_low[kind]
            tile = product(other, (c_high[:, own_half], c_low[:, own_half])).reshape(4, 4, 2, 8, SG)
            for half in range(2):
                pay[half, :, :, kinds + kind] = tile[:, :, half]
            for rank in range(2):
                at = pl.ds(rank * 256, 256)
                tile = product((c_high[at, own_half], c_low[at, own_half]), other).reshape(4, 4, 2, 8, 256)
                for half in range(2):
                    pay[half, :, :, kind, :, pl.ds(rank * 256, 256)] = tile[:, :, half]

    def reduce_scatter(pay, r0, r1, r2, r3, r4, tiles):
        span = tiles // 2

        def start(copy):
            copy.start()
            started.append(copy)
            return copy

        step = start(remote(pay.at[1 - core], r0, par_peer(y, zh, 1 - core)))
        yield
        step.wait_recv()
        r0[...] = r0[...] + pay[core]
        orders = ((1, 3), (3, 1))
        steps = []
        for q, (near, far) in enumerate(orders):
            at = pl.ds(q * span, span)
            peer = par_peer(flip(y, near, 2), zh, core)
            steps.append([
                start(remote(r0.at[flip(y, 2, 2), :, at], r1.at[q, 1], peer)),
                start(remote(r0.at[flip(y, near, 2), :, at], r1.at[q, 0], peer)),
            ])
        yield
        nexts = []
        for q, (near, far) in enumerate(orders):
            at = pl.ds(q * span, span)
            steps[q][0].wait_recv()
            r1[q, 1] = r1[q, 1] + r0[flip(y, far, 2), :, at]
            nexts.append(start(remote(r1.at[q, 1], r2.at[q], par_peer(flip(y, far, 2), zh, core))))
        for q in range(2):
            at = pl.ds(q * span, span)
            steps[q][1].wait_recv()
            r1[q, 0] = r1[q, 0] + r0[y, :, at]
        yield
        steps = []
        for q, (near, far) in enumerate(orders):
            nexts[q].wait_recv()
            r2[q] = r2[q] + r1[q, 0]
            peer = par_peer(y, flip(zh, near, 2), core)
            steps.append([
                start(remote(r2.at[q, flip(zh, 2, 2)], r3.at[q, 1], peer)),
                start(remote(r2.at[q, flip(zh, near, 2)], r3.at[q, 0], peer)),
            ])
        yield
        nexts = []
        for q, (near, far) in enumerate(orders):
            steps[q][0].wait_recv()
            r3[q, 1] = r3[q, 1] + r2[q, flip(zh, far, 2)]
            nexts.append(start(remote(r3.at[q, 1], r4.at[q], par_peer(y, flip(zh, far, 2), core))))
        for q in range(2):
            steps[q][1].wait_recv()
            r3[q, 0] = r3[q, 0] + r2[q, zh]
        yield
        for q in range(2):
            nexts[q].wait_recv()
            r4[q] = r4[q] + r3[q, 0]

    def reduce_chunk(c):
        yield from reduce_scatter(
            pay_c.at[c], r0_c.at[c], r1_c.at[c], r2_c.at[c], r3_c.at[c], r4_c.at[c], 2 * kinds
        )
        steps = []
        for kind, mask in enumerate((7, m)[:kinds]):
            copy = remote(r4_c.at[c, 1, kind], cross.at[c, kind], samp_peer(mask))
            copy.start()
            started.append(copy)
            steps.append(copy)
        yield
        for copy in steps:
            copy.wait_recv()

    def ordered(value, index):
        high, low = split(value)
        rest = value - high.astype(F32) - low.astype(F32)
        stacked = jnp.concatenate([high, low, rest.astype(BF16)], axis=0)
        moved = lax.dot_general(stacked, picks[index], (((1,), (0,)), ((), ())), preferred_element_type=F32)
        return (moved[0:16] + (moved[16:32] + moved[32:48])) * (1.0 / SAMPLES)

    def whole(kind):
        blocks = []
        for rank in range(2):
            at = pl.ds(rank * 256, 256)
            own = jnp.concatenate([r4_c[0, 0, kind, :, at], r4_c[1, 0, kind, :, at]], axis=1)
            blocks.append(own + cross[rank, kind])
        return jnp.concatenate(blocks, axis=0)

    exchange(0)
    diagonal()
    walk_d = reduce_scatter(pay_d, r0_d, r1_d, r2_d, r3_d, r4_d, 2)
    next(walk_d)
    for slot in range(1, PARTS + depth - 1):
        exchange(slot)
        if slot < 5:
            next(walk_d)
    chunk(0)
    walk_0 = reduce_chunk(0)
    next(walk_0)
    if depth == 2:
        next(walk_d, None)
    for slot in range(PARTS + depth - 1, SUBS + depth - 1):
        exchange(slot)
        next(walk_0)
        if slot == PARTS + depth - 1:
            for _ in walk_d:
                pass
    chunk(1)
    walk_1 = reduce_chunk(1)
    next(walk_1)
    tile_d = jnp.concatenate([r4_d[0, 0], r4_d[1, 0]], axis=0)
    out_ref[0, 0] = ordered(tile_d, 0)
    next(walk_0, None)
    next(walk_1)
    for _ in walk_0:
        pass
    for _ in walk_1:
        pass
    tile_7 = ordered(whole(0), 1)
    tile_m = ordered(tile_d if m == 0 else whole(1), 2)
    out_ref[0, 1] = jnp.where(seven_first, tile_7, tile_m)
    out_ref[0, 2] = jnp.where(seven_first, tile_m, tile_7)
    for copy in started:
        copy.wait_send()


def gram(m, x, spins, roster):
    kinds = 1 if m == 0 else 2
    span = kinds
    vmem = pltpu.VMEM
    scratch = [
        vmem((2, 32, 8, COLS), F32),
        vmem((2, 32, 8, HALF), F32),
        vmem((2, 32, 8, HALF), F32),
        vmem((2, 32, 8, HALF), F32),
        vmem((8, 1, COLS), F32),
        vmem((1, COLS), F32),
        vmem((SG, COLS), BF16),
        vmem((SG, COLS), BF16),
        vmem((2, 256, HALF), BF16),
        vmem((2, 256, HALF), BF16),
        vmem((2, 4, 4, 2, 8, SG), F32),
        vmem((2, 2, 4, 4, 2 * span, 8, SG), F32),
        vmem((4, 4, 2, 8, SG), F32),
        vmem((2, 4, 4, 2 * span, 8, SG), F32),
        vmem((2, 2, 4, 1, 8, SG), F32),
        vmem((2, 2, 2, 4, span, 8, SG), F32),
        vmem((2, 4, 1, 8, SG), F32),
        vmem((2, 2, 4, span, 8, SG), F32),
        vmem((2, 2, 1, 8, SG), F32),
        vmem((2, 2, 2, span, 8, SG), F32),
        vmem((2, 1, 8, SG), F32),
        vmem((2, 2, span, 8, SG), F32),
        vmem((2, 2, 8, SG), F32),
        vmem((3, SG, SG), BF16),
        pltpu.SemaphoreType.DMA((2,)),
        pltpu.SemaphoreType.DMA((80,)),
        pltpu.SemaphoreType.DMA((80,)),
    ]
    return pl.pallas_call(
        functools.partial(kernel, m),
        out_shape=jax.ShapeDtypeStruct((1, 3, 16, SG), F32),
        in_specs=[
            pl.BlockSpec(memory_space=pl.ANY),
            pl.BlockSpec(memory_space=pltpu.VMEM),
            pl.BlockSpec(memory_space=pltpu.VMEM),
        ],
        out_specs=pl.BlockSpec(memory_space=pltpu.VMEM),
        scratch_shapes=scratch,
        compiler_params=pltpu.CompilerParams(
            collective_id=m, has_side_effects=True, vmem_limit_bytes=48 * 1024 * 1024
        ),
        name=f"gram_{m}",
    )(x, spins, roster)


def on_device(log_derivs, spins, roster):
    x = log_derivs.reshape(32, 2, 8, COLS)
    spins = spins.reshape(32, 2, 8, NSITES)
    masks = roster[:, 0] // SG
    other = jnp.where(masks[0] == 7, masks[1], masks[0])
    return lax.switch(other, [functools.partial(gram, m) for m in range(7)], x, spins, roster)


def solution(mesh):
    in_specs = (P("samp", "par"), P("samp", None), P())
    out_specs = P("samp", None, "par", None)
    return jax.shard_map(
        on_device, mesh=mesh, in_specs=in_specs, out_specs=out_specs, check_vma=False
    )
```

```python
import functools

import jax
import jax.numpy as jnp
from jax import lax
from jax.experimental import pallas as pl
from jax.experimental.pallas import tpu as pltpu
from jax.sharding import PartitionSpec as P

MESH = pl.DeviceIdType.MESH
F32, BF16 = jnp.float32, jnp.bfloat16

SG = 512
NSITES = 100
LSIDE = 10
COLS = 1024
HALF = COLS // 2
SAMPLES = 4096
SUBS = 32
LAG = 5
SLOTS = SUBS + LAG
CHUNKS = 4


def bit_of(value, index):
    return lax.rem(lax.div(value, jnp.int32(2**index)), jnp.int32(2))


def flip(value, mask, bits):
    total = jnp.int32(0)
    for index in range(bits):
        bit = bit_of(value, index)
        total = total + (1 - bit if mask >> index & 1 else bit) * 2**index
    return total


def dot_nt(left, right):
    return lax.dot_general(left, right, (((1,), (1,)), ((), ())), preferred_element_type=F32)


def split(value):
    high = value.astype(BF16)
    return high, (value - high.astype(F32)).astype(BF16)


def product(left, right):
    (left_high, left_low), (right_high, right_low) = left, right
    return dot_nt(left_high, right_high) + (dot_nt(left_high, right_low) + dot_nt(left_low, right_high))


def kernel(x_hbm, spins_hbm, roster_hbm, out_ref, *scratch):
    (rows, spins_ref, roster_ref, own, stage_x, stage_z, stage_1, got_x, got_z, got_1, sums, mean_ref,
     c_high, c_low, h_high, h_low, b_high, b_low, pay_d, pay_a, pay_b, r0_d, r0_c, r1_d, r1_c,
     r2_d, r2_c, r3_d, r3_c, r4_d, r4_c, cross_7, cross_m, picks,
     load_sem, send_sem, recv_sem) = scratch
    group = lax.axis_index("samp")
    part = lax.axis_index("par")
    core = lax.rem(part, jnp.int32(2))
    zh = lax.rem(lax.div(part, jnp.int32(2)), jnp.int32(4))
    y = lax.div(part, jnp.int32(8))

    def samp_peer(mask):
        return {"samp": flip(group, mask, 3)}

    def par_peer(new_y, new_zh, new_core):
        return {"par": new_y * 8 + new_zh * 2 + new_core}

    sibling = par_peer(y, zh, 1 - core)
    load_spins = pltpu.make_async_copy(spins_hbm, spins_ref, load_sem.at[4])
    load_roster = pltpu.make_async_copy(roster_hbm, roster_ref, load_sem.at[5])
    loads = [
        pltpu.make_async_copy(x_hbm.at[:, :, k % 2, k // 2], rows.at[k], load_sem.at[k]) for k in range(CHUNKS)
    ]
    for load in (load_roster, load_spins, *loads):
        load.start()

    peers = [samp_peer(mask) for mask in range(7, 0, -1)]
    peers += [par_peer(y, flip(zh, mask, 2), core) for mask in (2, 1, 3)]
    peers += [par_peer(flip(y, mask, 2), zh, core) for mask in (1, 3)]
    peers += [sibling]
    barrier = pltpu.get_barrier_semaphore()
    for peer in peers:
        pl.semaphore_signal(barrier, inc=1, device_id=peer, device_id_type=MESH)

    counter = [0]
    open_sends = []

    def fresh():
        counter[0] += 1
        return counter[0] - 1

    def remote(src, dst, peer, index):
        return pltpu.make_async_remote_copy(
            src_ref=src, dst_ref=dst, send_sem=send_sem.at[index], recv_sem=recv_sem.at[index],
            device_id=peer, device_id_type=MESH,
        )

    def start(copy):
        copy.start()
        open_sends.append((None, copy))
        return copy

    def start_under(gate, copy):
        pl.when(gate)(copy.start)
        open_sends.append((gate, copy))
        return copy

    load_roster.wait()
    masks = lax.shift_right_logical(roster_ref[...], 9)
    within = roster_ref[...] & (SG - 1)
    seven_first = masks[0:1] == 7
    other = jnp.where(seven_first, masks[1:2], masks[0:1])
    bits = [bit_of(group, index) for index in range(3)]
    side = jnp.where(other == 4, bits[2], jnp.where((other == 2) | (other == 6), bits[1], bits[0]))
    m_part = jnp.broadcast_to(other, (16, SG))
    z_first = (m_part == 1) | (m_part == 3)

    load_spins.wait()
    site = lax.broadcasted_iota(jnp.int32, (NSITES, SG), 0)
    on_a = lax.rem(lax.div(site, jnp.int32(LSIDE)) + lax.rem(site, jnp.int32(LSIDE)), jnp.int32(2)) == 0
    count = jnp.sum(jnp.where(on_a, spins_ref[...], 0).astype(F32), axis=0, keepdims=True)
    sign_row = 1.0 - 2.0 * (count - 2.0 * jnp.floor(count * 0.5))
    sign = jnp.transpose(jnp.broadcast_to(sign_row, (128, SG)))[:, 0:1].reshape(4, 4, 2, 2, 8, 1)
    side128 = jnp.broadcast_to(side, (128, SG)) == 1
    column_sum = jnp.zeros((8, COLS), F32)
    for k in range(CHUNKS):
        loads[k].wait()
        signed = rows[k] * sign[:, :, k % 2, k // 2]
        rows[k] = signed
        column_sum = column_sum + jnp.sum(signed.reshape(16, 8, COLS), axis=0)
        flat = signed.reshape(128, COLS)
        own[pl.ds(8 * k, 8)] = jnp.where(side128, flat[:, :HALF], flat[:, HALF:]).reshape(8, 16, HALF)
    sums[0] = jnp.sum(column_sum, axis=0, keepdims=True)
    sum_copies = [remote(sums.at[0], sums.at[mask], samp_peer(mask), fresh()) for mask in range(1, 8)]

    hops = {"x": [], "z": [], "1": []}
    hop_masks = {"x": 6, "z": 1, "1": 2}
    hop_sems = {hop: [fresh() for _ in range(2 * LAG)] for hop in hops}

    def send_hop(hop, src, dst):
        sems, copies = hop_sems[hop], hops[hop]
        if len(copies) >= len(sems):
            copies[-len(sems)].wait_send()
        copy = remote(src, dst, samp_peer(hop_masks[hop]), sems[len(copies) % len(sems)])
        copy.start()
        copies.append(copy)

    def exchange(slot):
        before = slot - LAG
        if 0 <= before < SLOTS:
            for hop in "xz":
                hops[hop][before].wait_recv()
        if slot < SLOTS:
            if slot < LAG:
                from_x = from_z = own.at[slot]
            elif slot < SUBS:
                stage_x[slot] = jnp.where(z_first, got_z[before], own[slot])
                stage_z[slot] = jnp.where(z_first, own[slot], got_x[before])
                from_x, from_z = stage_x.at[slot], stage_z.at[slot]
            else:
                from_x, from_z = got_z.at[before], got_x.at[before]
            send_hop("x", from_x, got_x.at[slot])
            send_hop("z", from_z, got_z.at[slot])
        sub = slot - 3 * LAG
        if 0 <= sub < SUBS:
            hops["1"][sub].wait_recv()
        sub = slot - 2 * LAG
        if 0 <= sub < SUBS:
            stage_1[sub] = jnp.where(
                m_part == 2, own[sub],
                jnp.where(m_part == 3, got_z[sub], jnp.where(m_part == 4, got_x[sub], got_z[sub + LAG])),
            )
            send_hop("1", stage_1.at[sub], got_1.at[sub])

    natural = lax.broadcasted_iota(jnp.int32, (1, SG), 1)
    plans = [
        natural,
        jnp.where(seven_first, within[0:1], within[1:2]),
        jnp.where(seven_first, within[1:2], within[0:1]),
    ]

    def place_picks(index):
        plan = plans[index]
        p = plan >> 4
        place = ((plan >> 3) & 1) * 256 + (p & 1) * 128 + (p >> 3) * 32 + ((p >> 1) & 3) * 8 + (plan & 7)
        for first in range(0, SG, 128):
            position = lax.broadcasted_iota(jnp.int32, (128, SG), 0) + first
            picks[index, pl.ds(first, 128)] = jnp.where(position == place, 1.0, 0.0).astype(BF16)

    def centre():
        for copy in sum_copies:
            copy.wait_recv()
        mean = (
            ((sums[0] + sums[1]) + (sums[2] + sums[3])) + ((sums[4] + sums[5]) + (sums[6] + sums[7]))
        ) * (1.0 / SAMPLES)
        mean_ref[...] = jnp.where(side == 1, mean[:, HALF:], mean[:, :HALF])
        for k in range(CHUNKS):
            at = pl.ds(k * 128, 128)
            centred = rows[k].reshape(128, COLS) - mean
            c_high[at], c_low[at] = split(centred)
            h_high[at], h_low[at] = split(jnp.where(side128, centred[:, HALF:], centred[:, :HALF]))

    order_of = ((0, 3, 1, 2), (0, 1, 2, 3))
    hop_pairs = ((1, 3), (3, 1))

    def pair_of(index, q):
        low, high = bit_of(index, 0), bit_of(index, 1)
        return lax.rem(low + high, jnp.int32(2)) if q == 0 else high

    def place_in(index, q):
        return bit_of(index, 1 - q)

    def diagonal(index):
        at = pl.ds(index * 256, 256)
        tile = product((c_high[...], c_low[...]), (c_high[at], c_low[at])).reshape(2, 2, 4, 4, 8, 256)
        for c in range(2):
            for i, to_y in enumerate(order_of[c]):
                for to_zh in range(4):
                    pay_d[:, c, i, to_zh, :, at] = tile[c, :, to_y, to_zh]

    def gather(k, kind):
        for j in range(8):
            sub = 8 * k + j
            if kind == 0:
                part_rows = jnp.where(z_first, got_x[sub + LAG], got_z[sub + LAG])
            else:
                part_rows = jnp.where(m_part == 1, got_z[sub], jnp.where(m_part == 6, got_x[sub], got_1[sub]))
            at = pl.ds(kind * 128 + 16 * j, 16)
            b_high[at], b_low[at] = split(part_rows - mean_ref[...])

    def tiles_back(k):
        tile = product((b_high[...], b_low[...]), (h_high[...], h_low[...])).reshape(2, 4, 4, 8, SG)
        for q in range(2):
            for i, to_y in enumerate(order_of[q]):
                for to_zh in range(4):
                    pay_b[k, q, i, to_zh] = tile[q, to_y, to_zh]

    def tiles_own(k):
        tile = product((h_high[...], h_low[...]), (b_high[...], b_low[...])).reshape(2, 2, 4, 4, 8, 256)
        for q in range(2):
            for i, to_y in enumerate(order_of[q]):
                for to_zh in range(4):
                    for c in range(2):
                        pay_a[k, :, q, i, to_zh, :, pl.ds(c * 128, 128)] = tile[c, :, to_y, to_zh, :, q * 128 : q * 128 + 128]

    def halving(r0, r1, r2, r3, r4, wide):
        def hop(src, dst, peer):
            index = fresh()
            if wide is None:
                return [(None, start(remote(src, dst, peer, index)))]
            first = pl.ds(0, 256)
            narrow = remote(src.at[..., first], dst.at[..., first], peer, index)
            return [
                (wide[0], start_under(wide[0], remote(src, dst, peer, index))),
                (wide[1], start_under(wide[1], narrow)),
            ]

        def arrive(copies):
            for gate, copy in copies:
                if gate is None:
                    copy.wait_recv()
                else:
                    pl.when(gate)(copy.wait_recv)

        def add(dst, at, other):
            if wide is None:
                dst[at] = dst[at] + other[...]
                return
            first, rest = pl.ds(0, 256), pl.ds(256, SG)
            dst[at + (Ellipsis, first)] = dst[at + (Ellipsis, first)] + other[..., first]

            @pl.when(wide[0])
            def _():
                dst[at + (Ellipsis, rest)] = dst[at + (Ellipsis, rest)] + other[..., rest]

        steps = []
        for q, (near, _) in enumerate(hop_pairs):
            peer = par_peer(flip(y, near, 2), zh, core)
            steps.append(hop(r0.at[q, pl.ds(2 * (1 - pair_of(y, q)), 2)], r1.at[q], peer))
        yield
        nexts = []
        for q, (_, far) in enumerate(hop_pairs):
            pair, place = pair_of(y, q), place_in(y, q)
            arrive(steps[q])
            add(r1, (q, 1 - place), r0.at[q, 2 * pair + 1 - place])
            nexts.append(hop(r1.at[q, 1 - place], r2.at[q], par_peer(flip(y, far, 2), zh, core)))
        for q in range(2):
            pair, place = pair_of(y, q), place_in(y, q)
            add(r1, (q, place), r0.at[q, 2 * pair + place])
        yield
        steps = []
        for q in range(2):
            arrive(nexts[q])
            add(r2, (q,), r1.at[q, place_in(y, q)])
        for mask in (2, 1, 3):
            to = flip(zh, mask, 2)
            steps.append(hop(r2.at[:, to], r3.at[mask - 1], par_peer(y, to, core)))
        yield
        for copies in steps:
            arrive(copies)
        r4[...] = (r2[:, zh] + r3[0]) + (r3[1] + r3[2])

    def reduce_diagonal():
        step = start(remote(pay_d.at[1 - core], r0_d, sibling, fresh()))
        yield
        step.wait_recv()
        r0_d[...] = r0_d[...] + pay_d[core]
        yield from halving(r0_d, r1_d, r2_d, r3_d, r4_d, None)

    back_sems = [fresh() for _ in range(2)]
    cross_sems = [[fresh() for _ in range(7)] for _ in range(2)]

    def reduce_chunk(k):
        c, to = k // 2, k % 2
        here, there = core == to, core != to
        first, rest = pl.ds(0, 256), pl.ds(256, SG)
        step_a = start(remote(pay_a.at[k, 1 - core], r0_c.at[k, ..., first], sibling, fresh()))
        step_b = start_under(there, remote(pay_b.at[k], r0_c.at[k, ..., rest], sibling, back_sems[c]))
        yield
        step_a.wait_recv()
        r0_c[k, ..., first] = r0_c[k, ..., first] + pay_a[k, core]

        @pl.when(here)
        def _():
            step_b.wait_recv()
            r0_c[k, ..., rest] = r0_c[k, ..., rest] + pay_b[k]

        yield from halving(r0_c.at[k], r1_c.at[k], r2_c.at[k], r3_c.at[k], r4_c.at[k], (here, there))
        crossings = [start_under(here, remote(r4_c.at[k, 0, :, rest], cross_7.at[c], samp_peer(7), cross_sems[c][0]))]
        for mask in range(1, 7):
            crossings.append(start_under(
                here, remote(r4_c.at[k, 1, :, rest], cross_m.at[c, mask - 1], samp_peer(mask), cross_sems[c][mask])
            ))
        yield

        @pl.when(here)
        def _():
            for copy in crossings:
                copy.wait_recv()

    def ordered(value, index):
        high, low = split(value)
        rest = value - high.astype(F32) - low.astype(F32)
        stacked = jnp.concatenate([high, low, rest.astype(BF16)], axis=0)
        moved = lax.dot_general(stacked, picks[index], (((1,), (0,)), ((), ())), preferred_element_type=F32)
        return (moved[0:16] + (moved[16:32] + moved[32:48])) * (1.0 / SAMPLES)

    def whole(kind):
        blocks = []
        for c in range(2):
            own_part = jnp.concatenate([r4_c[k, kind, :, pl.ds(c * 128, 128)] for k in range(CHUNKS)], axis=1)
            if kind == 0:
                arrived = cross_7[c]
            else:
                arrived = cross_m[c, 0]
                for mask in range(2, 7):
                    arrived = jnp.where(other == mask, cross_m[c, mask - 1], arrived)
            blocks.append(own_part + arrived)
        return jnp.concatenate(blocks, axis=0)

    def scope(name):
        return jax.named_scope(name)

    walks = {}

    def advance(name):
        next(walks[name], None)

    def begin(name, walk):
        walks[name] = walk
        advance(name)

    def make_d(index):
        diagonal(index)
        if index == 1:
            begin("d", reduce_diagonal())

    def back(k):
        gather(k, 1)
        tiles_back(k)

    def make(k):
        tiles_own(k)
        begin(k, reduce_chunk(k))

    with scope("bar"):
        pl.semaphore_wait(barrier, len(peers))
    for copy in sum_copies:
        start(copy)
    after = {
        0: [(place_picks, 0)],
        1: [(place_picks, 1)],
        2: [(place_picks, 2)],
        7: [(centre,)],
        8: [(make_d, 0)],
        10: [(make_d, 1)],
        18: [(advance, "d"), (gather, 0, 0)],
        22: [(back, 0)],
        23: [(make, 0)],
        25: [(advance, "d"), (gather, 1, 0)],
        30: [(back, 1)],
        31: [(make, 1), (advance, 0), (advance, "d")],
        33: [(gather, 2, 0)],
        37: [(advance, "d")],
        38: [(back, 2), (advance, 0)],
        39: [(make, 2), (advance, 1)],
        41: [(gather, 3, 0)],
        44: [(advance, 0)],
        45: [(advance, 1)],
        46: [(back, 3), (make, 3)],
    }
    for slot in range(SUBS + 3 * LAG):
        with scope(f"ex{slot}"):
            exchange(slot)
        for job, *about in after.get(slot, []):
            with scope(f"job{slot}_{job.__name__}_{about}"):
                job(*about)
    for _ in walks["d"]:
        pass
    with scope("tile_d"):
        tile_d = jnp.concatenate([r4_d[0], r4_d[1]], axis=0)
        out_ref[0, 0] = ordered(tile_d, 0)
    for turn in range(7):
        for name in (0, 1, 2, 3):
            with scope(f"tail{turn}_{name}"):
                advance(name)
    with scope("final"):
        tile_7 = ordered(whole(0), 1)
        tile_m = ordered(jnp.where(other == 0, tile_d, whole(1)), 2)
        out_ref[0, 1] = jnp.where(seven_first, tile_7, tile_m)
        out_ref[0, 2] = jnp.where(seven_first, tile_m, tile_7)
    with scope("drain"):
        for hop, copies in hops.items():
            for copy in copies[-len(hop_sems[hop]):]:
                copy.wait_send()
        for gate, copy in open_sends:
            if gate is None:
                copy.wait_send()
            else:
                pl.when(gate)(copy.wait_send)


def gram(x, spins, roster):
    vmem = pltpu.VMEM

    def halves(lead, width):
        return [
            vmem(lead + (2, 4, 4, 8, width), F32),
            vmem(lead + (2, 2, 4, 8, width), F32),
            vmem(lead + (2, 4, 8, width), F32),
            vmem(lead + (3, 2, 8, width), F32),
            vmem(lead + (2, 8, width), F32),
        ]

    sets = [halves((), SG), halves((CHUNKS,), 256 + SG)]
    scratch = [
        vmem((CHUNKS, 4, 4, 8, COLS), F32),
        vmem((NSITES, SG), jnp.int32),
        vmem((2, SG), jnp.int32),
        vmem((SUBS, 16, HALF), F32),
        vmem((SLOTS, 16, HALF), F32),
        vmem((SLOTS, 16, HALF), F32),
        vmem((SUBS, 16, HALF), F32),
        vmem((SLOTS, 16, HALF), F32),
        vmem((SLOTS, 16, HALF), F32),
        vmem((SUBS, 16, HALF), F32),
        vmem((8, 1, COLS), F32),
        vmem((1, HALF), F32),
        vmem((SG, COLS), BF16),
        vmem((SG, COLS), BF16),
        vmem((SG, HALF), BF16),
        vmem((SG, HALF), BF16),
        vmem((256, HALF), BF16),
        vmem((256, HALF), BF16),
        vmem((2, 2, 4, 4, 8, SG), F32),
        vmem((CHUNKS, 2, 2, 4, 4, 8, 256), F32),
        vmem((CHUNKS, 2, 4, 4, 8, SG), F32),
        *[one[step] for step in range(5) for one in sets],
        vmem((2, 8, SG), F32),
        vmem((2, 6, 8, SG), F32),
        vmem((3, SG, SG), BF16),
        pltpu.SemaphoreType.DMA((6,)),
        pltpu.SemaphoreType.DMA((98,)),
        pltpu.SemaphoreType.DMA((98,)),
    ]
    return pl.pallas_call(
        kernel,
        out_shape=jax.ShapeDtypeStruct((1, 3, 16, SG), F32),
        in_specs=[pl.BlockSpec(memory_space=pltpu.HBM)] * 3,
        out_specs=pl.BlockSpec(memory_space=pltpu.VMEM),
        scratch_shapes=scratch,
        compiler_params=pltpu.CompilerParams(
            collective_id=0, has_side_effects=True, vmem_limit_bytes=56 * 1024 * 1024
        ),
        name="gram",
    )(x, spins, roster)


def on_device(log_derivs, spins, roster):
    return gram(log_derivs.reshape(4, 4, 2, 2, 8, COLS), spins.T, roster)


def solution(mesh):
    in_specs = (P("samp", "par"), P("samp", None), P())
    out_specs = P("samp", None, "par", None)
    return jax.shard_map(
        on_device, mesh=mesh, in_specs=in_specs, out_specs=out_specs, check_vma=False
    )
```

```python
import functools

import jax
import jax.numpy as jnp
from jax import lax
from jax.experimental import pallas as pl
from jax.experimental.pallas import tpu as pltpu
from jax.sharding import PartitionSpec as P

MESH = pl.DeviceIdType.MESH
F32, BF16 = jnp.float32, jnp.bfloat16

SG = 512
NSITES = 100
LSIDE = 10
COLS = 1024
HALF = COLS // 2
SAMPLES = 4096
SUBS = 32
LAG = 6
SLOTS = SUBS + LAG
LAST = 5
CHUNKS = 4


def bit_of(value, index):
    return lax.rem(lax.div(value, jnp.int32(2**index)), jnp.int32(2))


def flip(value, mask, bits):
    total = jnp.int32(0)
    for index in range(bits):
        bit = bit_of(value, index)
        total = total + (1 - bit if mask >> index & 1 else bit) * 2**index
    return total


def dot_nt(left, right):
    return lax.dot_general(left, right, (((1,), (1,)), ((), ())), preferred_element_type=F32)


def split(value):
    high = value.astype(BF16)
    return high, (value - high.astype(F32)).astype(BF16)


def product(left, right):
    (left_high, left_low), (right_high, right_low) = left, right
    return dot_nt(left_high, right_high) + (dot_nt(left_high, right_low) + dot_nt(left_low, right_high))


def kernel(x_hbm, spins_hbm, roster_hbm, out_ref, *scratch):
    (rows, spins_ref, roster_ref, own, stage_x, stage_z, stage_1, got_x, got_z, got_1, sums, mean_ref,
     c_high, c_low, h_high, h_low, b_high, b_low, pay_d, pay_a, pay_b, r0_d, r0_c, r1_d, r1_c,
     r2_d, r2_c, r3_d, r3_c, r4_d, r4_c, cross_7, cross_m, picks,
     load_sem, send_sem, recv_sem) = scratch
    group = lax.axis_index("samp")
    part = lax.axis_index("par")
    core = lax.rem(part, jnp.int32(2))
    zh = lax.rem(lax.div(part, jnp.int32(2)), jnp.int32(4))
    y = lax.div(part, jnp.int32(8))

    def samp_peer(mask):
        return {"samp": flip(group, mask, 3)}

    def par_peer(new_y, new_zh, new_core):
        return {"par": new_y * 8 + new_zh * 2 + new_core}

    sibling = par_peer(y, zh, 1 - core)
    load_spins = pltpu.make_async_copy(spins_hbm, spins_ref, load_sem.at[4])
    load_roster = pltpu.make_async_copy(roster_hbm, roster_ref, load_sem.at[5])
    loads = [
        pltpu.make_async_copy(x_hbm.at[:, :, k % 2, k // 2], rows.at[k], load_sem.at[k]) for k in range(CHUNKS)
    ]
    for load in (load_roster, load_spins, *loads):
        load.start()

    peers = [samp_peer(mask) for mask in range(7, 0, -1)]
    peers += [par_peer(y, flip(zh, mask, 2), core) for mask in (1, 3)]
    peers += [par_peer(flip(y, mask, 2), zh, core) for mask in (1, 3)]
    peers += [sibling]
    barrier = pltpu.get_barrier_semaphore()
    for peer in peers:
        pl.semaphore_signal(barrier, inc=1, device_id=peer, device_id_type=MESH)

    counter = [0]
    open_sends = []

    def fresh():
        counter[0] += 1
        return counter[0] - 1

    def remote(src, dst, peer, index):
        return pltpu.make_async_remote_copy(
            src_ref=src, dst_ref=dst, send_sem=send_sem.at[index], recv_sem=recv_sem.at[index],
            device_id=peer, device_id_type=MESH,
        )

    def start(copy):
        copy.start()
        open_sends.append((None, copy))
        return copy

    def start_under(gate, copy):
        pl.when(gate)(copy.start)
        open_sends.append((gate, copy))
        return copy

    load_roster.wait()
    masks = lax.shift_right_logical(roster_ref[...], 9)
    within = roster_ref[...] & (SG - 1)
    seven_first = masks[0:1] == 7
    other = jnp.where(seven_first, masks[1:2], masks[0:1])
    bits = [bit_of(group, index) for index in range(3)]
    side = jnp.where(other == 4, bits[2], jnp.where((other == 2) | (other == 6), bits[1], bits[0]))
    m_part = jnp.broadcast_to(other, (16, SG))
    z_first = (m_part == 1) | (m_part == 3)

    load_spins.wait()
    site = lax.broadcasted_iota(jnp.int32, (NSITES, SG), 0)
    on_a = lax.rem(lax.div(site, jnp.int32(LSIDE)) + lax.rem(site, jnp.int32(LSIDE)), jnp.int32(2)) == 0
    count = jnp.sum(jnp.where(on_a, spins_ref[...], 0).astype(F32), axis=0, keepdims=True)
    sign_row = 1.0 - 2.0 * (count - 2.0 * jnp.floor(count * 0.5))
    sign = jnp.transpose(jnp.broadcast_to(sign_row, (128, SG)))[:, 0:1].reshape(4, 4, 2, 2, 8, 1)
    side128 = jnp.broadcast_to(side, (128, SG)) == 1
    column_sum = jnp.zeros((8, COLS), F32)
    for k in range(CHUNKS):
        loads[k].wait()
        signed = rows[k] * sign[:, :, k % 2, k // 2]
        rows[k] = signed
        column_sum = column_sum + jnp.sum(signed.reshape(16, 8, COLS), axis=0)
        flat = signed.reshape(128, COLS)
        own[pl.ds(8 * k, 8)] = jnp.where(side128, flat[:, :HALF], flat[:, HALF:]).reshape(8, 16, HALF)
    sums[0] = jnp.sum(column_sum, axis=0, keepdims=True)
    sum_copies = [remote(sums.at[0], sums.at[mask], samp_peer(mask), fresh()) for mask in range(1, 8)]

    hops = {"x": [], "z": [], "1": []}
    hop_masks = {"x": 6, "z": 1, "1": 2}
    hop_sems = {hop: [fresh() for _ in range(2 * (LAST if hop == "1" else LAG))] for hop in hops}

    def send_hop(hop, src, dst):
        sems, copies = hop_sems[hop], hops[hop]
        if len(copies) >= len(sems):
            copies[-len(sems)].wait_send()
        copy = remote(src, dst, samp_peer(hop_masks[hop]), sems[len(copies) % len(sems)])
        copy.start()
        copies.append(copy)

    def exchange(slot):
        before = slot - LAG
        if 0 <= before < SLOTS:
            for hop in "xz":
                hops[hop][before].wait_recv()
        if slot < SLOTS:
            if slot < LAG:
                from_x = from_z = own.at[slot]
            elif slot < SUBS:
                stage_x[slot] = jnp.where(z_first, got_z[before], own[slot])
                stage_z[slot] = jnp.where(z_first, own[slot], got_x[before])
                from_x, from_z = stage_x.at[slot], stage_z.at[slot]
            else:
                from_x, from_z = got_z.at[before], got_x.at[before]
            send_hop("x", from_x, got_x.at[slot])
            send_hop("z", from_z, got_z.at[slot])
        sub = slot - 2 * LAG - LAST
        for sub in range(sub, sub + 1) if slot < SUBS + 2 * LAG else range(sub, SUBS):
            if sub >= 0:
                hops["1"][sub].wait_recv()
        sub = slot - 2 * LAG
        if 0 <= sub < SUBS:
            stage_1[sub] = jnp.where(
                m_part == 2, own[sub],
                jnp.where(m_part == 3, got_z[sub], jnp.where(m_part == 4, got_x[sub], got_z[sub + LAG])),
            )
            send_hop("1", stage_1.at[sub], got_1.at[sub])

    natural = lax.broadcasted_iota(jnp.int32, (1, SG), 1)
    plans = [
        natural,
        jnp.where(seven_first, within[0:1], within[1:2]),
        jnp.where(seven_first, within[1:2], within[0:1]),
    ]

    def place_picks(index):
        plan = plans[index]
        p = plan >> 4
        place = ((plan >> 3) & 1) * 256 + (p & 1) * 128 + (p >> 3) * 32 + ((p >> 1) & 3) * 8 + (plan & 7)
        for first in range(0, SG, 128):
            position = lax.broadcasted_iota(jnp.int32, (128, SG), 0) + first
            picks[index, pl.ds(first, 128)] = jnp.where(position == place, 1.0, 0.0).astype(BF16)

    def centre():
        for copy in sum_copies:
            copy.wait_recv()
        mean = (
            ((sums[0] + sums[1]) + (sums[2] + sums[3])) + ((sums[4] + sums[5]) + (sums[6] + sums[7]))
        ) * (1.0 / SAMPLES)
        mean_ref[...] = jnp.where(side == 1, mean[:, HALF:], mean[:, :HALF])
        for k in range(CHUNKS):
            at = pl.ds(k * 128, 128)
            centred = rows[k].reshape(128, COLS) - mean
            c_high[at], c_low[at] = split(centred)
            h_high[at], h_low[at] = split(jnp.where(side128, centred[:, HALF:], centred[:, :HALF]))

    order_of = ((0, 3, 1, 2), (0, 1, 2, 3))
    hop_pairs = ((1, 3), (3, 1))

    def pair_of(index, q):
        low, high = bit_of(index, 0), bit_of(index, 1)
        return lax.rem(low + high, jnp.int32(2)) if q == 0 else high

    def place_in(index, q):
        return bit_of(index, 1 - q)

    def diagonal(index):
        at = pl.ds(index * 256, 256)
        tile = product((c_high[...], c_low[...]), (c_high[at], c_low[at])).reshape(2, 2, 4, 4, 8, 256)
        for c in range(2):
            for i, to_y in enumerate(order_of[c]):
                for j, to_zh in enumerate(order_of[c]):
                    pay_d[:, c, i, j, :, at] = tile[c, :, to_y, to_zh]

    def gather(k, kind):
        for j in range(8):
            sub = 8 * k + j
            if kind == 0:
                part_rows = jnp.where(z_first, got_x[sub + LAG], got_z[sub + LAG])
            else:
                part_rows = jnp.where(m_part == 1, got_z[sub], jnp.where(m_part == 6, got_x[sub], got_1[sub]))
            at = pl.ds(kind * 128 + 16 * j, 16)
            b_high[at], b_low[at] = split(part_rows - mean_ref[...])

    def tiles(k, kinds):
        at = pl.ds(kinds[0] * 128, len(kinds) * 128)
        tile = product((h_high[...], h_low[...]), (b_high[at], b_low[at]))
        own_tile = tile.reshape(2, 2, 4, 4, 8, len(kinds) * 128)
        back_tile = jnp.transpose(tile).reshape(len(kinds), 4, 4, 8, SG)
        for index, q in enumerate(kinds):
            lanes = slice(index * 128, index * 128 + 128)
            for i, to_y in enumerate(order_of[q]):
                for j, to_zh in enumerate(order_of[q]):
                    pay_b[k, q, i, j] = back_tile[index, to_y, to_zh]
                    for c in range(2):
                        pay_a[k, :, q, i, j, :, pl.ds(c * 128, 128)] = own_tile[c, :, to_y, to_zh, :, lanes]

    def halving(r0, r1, r2, r3, r4, wide, qs=(0, 1)):
        def hop(src, dst, peer):
            index = fresh()
            if wide is None:
                return [(None, start(remote(src, dst, peer, index)))]
            first = pl.ds(0, 256)
            narrow = remote(src.at[..., first], dst.at[..., first], peer, index)
            return [
                (wide[0], start_under(wide[0], remote(src, dst, peer, index))),
                (wide[1], start_under(wide[1], narrow)),
            ]

        def arrive(copies):
            for gate, copy in copies:
                if gate is None:
                    copy.wait_recv()
                else:
                    pl.when(gate)(copy.wait_recv)

        def add(dst, at, other):
            if wide is None:
                dst[at] = dst[at] + other[...]
                return
            first, rest = pl.ds(0, 256), pl.ds(256, SG)
            dst[at + (Ellipsis, first)] = dst[at + (Ellipsis, first)] + other[..., first]

            @pl.when(wide[0])
            def _():
                dst[at + (Ellipsis, rest)] = dst[at + (Ellipsis, rest)] + other[..., rest]

        steps = {}
        for q in qs:
            near = hop_pairs[q][0]
            peer = par_peer(flip(y, near, 2), zh, core)
            steps[q] = hop(r0.at[q, pl.ds(2 * (1 - pair_of(y, q)), 2)], r1.at[q], peer)
        yield
        nexts = {}
        for q in qs:
            far = hop_pairs[q][1]
            pair, place = pair_of(y, q), place_in(y, q)
            arrive(steps[q])
            add(r1, (q, 1 - place), r0.at[q, 2 * pair + 1 - place])
            nexts[q] = hop(r1.at[q, 1 - place], r2.at[q], par_peer(flip(y, far, 2), zh, core))
        for q in qs:
            pair, place = pair_of(y, q), place_in(y, q)
            add(r1, (q, place), r0.at[q, 2 * pair + place])
        yield
        steps = {}
        for q in qs:
            near = hop_pairs[q][0]
            arrive(nexts[q])
            add(r2, (q,), r1.at[q, place_in(y, q)])
            peer = par_peer(y, flip(zh, near, 2), core)
            steps[q] = hop(r2.at[q, pl.ds(2 * (1 - pair_of(zh, q)), 2)], r3.at[q], peer)
        yield
        nexts = {}
        for q in qs:
            far = hop_pairs[q][1]
            pair, place = pair_of(zh, q), place_in(zh, q)
            arrive(steps[q])
            add(r3, (q, 1 - place), r2.at[q, 2 * pair + 1 - place])
            nexts[q] = hop(r3.at[q, 1 - place], r4.at[q], par_peer(y, flip(zh, far, 2), core))
        for q in qs:
            pair, place = pair_of(zh, q), place_in(zh, q)
            add(r3, (q, place), r2.at[q, 2 * pair + place])
        yield
        for q in qs:
            arrive(nexts[q])
            add(r4, (q,), r3.at[q, place_in(zh, q)])

    def reduce_diagonal():
        step = start(remote(pay_d.at[1 - core], r0_d, sibling, fresh()))
        yield
        step.wait_recv()
        r0_d[...] = r0_d[...] + pay_d[core]
        yield from halving(r0_d, r1_d, r2_d, r3_d, r4_d, None)

    cross_sems = [[fresh() for _ in range(7)] for _ in range(2)]

    def reduce_chunk(k, kinds):
        c, to = k // 2, k % 2
        here, there = core == to, core != to
        first, rest = pl.ds(0, 256), pl.ds(256, SG)
        at = pl.ds(kinds[0], len(kinds))
        step_a = start(remote(pay_a.at[k, 1 - core, at], r0_c.at[k, at, ..., first], sibling, fresh()))
        step_b = start_under(there, remote(pay_b.at[k, at], r0_c.at[k, at, ..., rest], sibling, fresh()))
        yield
        step_a.wait_recv()
        r0_c[k, at, ..., first] = r0_c[k, at, ..., first] + pay_a[k, core, at]

        @pl.when(here)
        def _():
            step_b.wait_recv()
            r0_c[k, at, ..., rest] = r0_c[k, at, ..., rest] + pay_b[k, at]

        yield from halving(r0_c.at[k], r1_c.at[k], r2_c.at[k], r3_c.at[k], r4_c.at[k], (here, there), kinds)
        crossings = []
        for kind in kinds:
            for mask in (7,) if kind == 0 else range(1, 7):
                to_ref = cross_7.at[c] if kind == 0 else cross_m.at[c, mask - 1]
                crossings.append(start_under(
                    here, remote(r4_c.at[k, kind, :, rest], to_ref, samp_peer(mask), cross_sems[c][mask - 1])
                ))
        yield

        @pl.when(here)
        def _():
            for copy in crossings:
                copy.wait_recv()

    def ordered(value, index):
        value = value * (1.0 / SAMPLES)
        high, low = split(value)
        rest = value - high.astype(F32) - low.astype(F32)
        stacked = jnp.concatenate([high, low, rest.astype(BF16)], axis=0)
        moved = lax.dot_general(stacked, picks[index], (((1,), (0,)), ((), ())), preferred_element_type=F32)
        return moved[0:16] + (moved[16:32] + moved[32:48])

    def whole(kind):
        blocks = []
        for c in range(2):
            own_part = jnp.concatenate([r4_c[k, kind, :, pl.ds(c * 128, 128)] for k in range(CHUNKS)], axis=1)
            if kind == 0:
                arrived = cross_7[c]
            else:
                arrived = cross_m[c, 0]
                for mask in range(2, 7):
                    arrived = jnp.where(other == mask, cross_m[c, mask - 1], arrived)
            blocks.append(own_part + arrived)
        return jnp.concatenate(blocks, axis=0)

    def scope(name):
        return jax.named_scope(name)

    walks = {}

    def advance(name):
        next(walks[name], None)

    def begin(name, walk):
        walks[name] = walk
        advance(name)

    def make_d(index):
        diagonal(index)
        if index == 1:
            begin("d", reduce_diagonal())

    both = (0, 1)

    def make(k, kinds):
        for kind in kinds:
            gather(k, kind)
        tiles(k, kinds)
        begin((k, kinds), reduce_chunk(k, kinds))

    with scope("bar"):
        pl.semaphore_wait(barrier, len(peers))
    for copy in sum_copies:
        start(copy)
    c0, c1, c2, c3 = ((k, both) for k in range(4))
    after = {
        0: [(place_picks, 0)],
        1: [(place_picks, 1)],
        2: [(place_picks, 2)],
        7: [(centre,)],
        9: [(make_d, 0)],
        14: [(make_d, 1)],
        22: [(advance, "d")],
        24: [(make, 0, both)],
        29: [(advance, "d")],
        30: [(advance, c0)],
        32: [(make, 1, both)],
        36: [(advance, c0), (advance, c1)],
        39: [(advance, "d")],
        43: [(make, 2, both), (advance, c0), (advance, c1), (advance, c2)],
        44: [(make, 3, both)],
    }
    for slot in range(SUBS + 2 * LAG + 1):
        with scope(f"ex{slot}"):
            exchange(slot)
        for job, *about in after.get(slot, []):
            with scope(f"job{slot}_{job.__name__}_{about}"):
                job(*about)
    def finish_d():
        tile_d = jnp.concatenate([r4_d[0], r4_d[1]], axis=0)
        out_ref[0, 0] = ordered(tile_d, 0)
        return tile_d
    for turn, name in enumerate((c3, c1, "d", c0, c2, c3, "d", "tile", c1, c0, c2, c3, c1, c2, c3, c2, c3, c0, c1, c2, c3)):
        with scope(f"tail{turn}_{name}"):
            if name == "tile":
                tile_d = finish_d()
            else:
                advance(name)
    with scope("final"):
        tile_7 = ordered(whole(0), 1)
        tile_m = ordered(jnp.where(other == 0, tile_d, whole(1)), 2)
        out_ref[0, 1] = jnp.where(seven_first, tile_7, tile_m)
        out_ref[0, 2] = jnp.where(seven_first, tile_m, tile_7)
    with scope("drain"):
        for hop, copies in hops.items():
            for copy in copies[-len(hop_sems[hop]):]:
                copy.wait_send()
        for gate, copy in open_sends:
            if gate is None:
                copy.wait_send()
            else:
                pl.when(gate)(copy.wait_send)


def gram(x, spins, roster):
    vmem = pltpu.VMEM

    def halves(lead, width):
        return [
            vmem(lead + (2, 4, 4, 8, width), F32),
            vmem(lead + (2, 2, 4, 8, width), F32),
            vmem(lead + (2, 4, 8, width), F32),
            vmem(lead + (2, 2, 8, width), F32),
            vmem(lead + (2, 8, width), F32),
        ]

    sets = [halves((), SG), halves((CHUNKS,), 256 + SG)]
    scratch = [
        vmem((CHUNKS, 4, 4, 8, COLS), F32),
        vmem((NSITES, SG), jnp.int32),
        vmem((2, SG), jnp.int32),
        vmem((SUBS, 16, HALF), F32),
        vmem((SLOTS, 16, HALF), F32),
        vmem((SLOTS, 16, HALF), F32),
        vmem((SUBS, 16, HALF), F32),
        vmem((SLOTS, 16, HALF), F32),
        vmem((SLOTS, 16, HALF), F32),
        vmem((SUBS, 16, HALF), F32),
        vmem((8, 1, COLS), F32),
        vmem((1, HALF), F32),
        vmem((SG, COLS), BF16),
        vmem((SG, COLS), BF16),
        vmem((SG, HALF), BF16),
        vmem((SG, HALF), BF16),
        vmem((256, HALF), BF16),
        vmem((256, HALF), BF16),
        vmem((2, 2, 4, 4, 8, SG), F32),
        vmem((CHUNKS, 2, 2, 4, 4, 8, 256), F32),
        vmem((CHUNKS, 2, 4, 4, 8, SG), F32),
        *[one[step] for step in range(5) for one in sets],
        vmem((2, 8, SG), F32),
        vmem((2, 6, 8, SG), F32),
        vmem((3, SG, SG), BF16),
        pltpu.SemaphoreType.DMA((6,)),
        pltpu.SemaphoreType.DMA((104,)),
        pltpu.SemaphoreType.DMA((104,)),
    ]
    return pl.pallas_call(
        kernel,
        out_shape=jax.ShapeDtypeStruct((1, 3, 16, SG), F32),
        in_specs=[pl.BlockSpec(memory_space=pltpu.HBM)] * 3,
        out_specs=pl.BlockSpec(memory_space=pltpu.VMEM),
        scratch_shapes=scratch,
        compiler_params=pltpu.CompilerParams(
            collective_id=0, has_side_effects=True, vmem_limit_bytes=56 * 1024 * 1024
        ),
        name="gram",
    )(x, spins, roster)


def on_device(log_derivs, spins, roster):
    return gram(log_derivs.reshape(4, 4, 2, 2, 8, COLS), spins.T, roster)


def solution(mesh):
    in_specs = (P("samp", "par"), P("samp", None), P())
    out_specs = P("samp", None, "par", None)
    return jax.shard_map(
        on_device, mesh=mesh, in_specs=in_specs, out_specs=out_specs, check_vma=False
    )
```

```python
import functools

import jax
import jax.numpy as jnp
from jax import lax
from jax.experimental import pallas as pl
from jax.experimental.pallas import tpu as pltpu
from jax.sharding import PartitionSpec as P

MESH = pl.DeviceIdType.MESH
F32, BF16 = jnp.float32, jnp.bfloat16

SG = 512
NSITES = 100
LSIDE = 10
COLS = 1024
HALF = COLS // 2
SAMPLES = 4096
SUBS = 32
LAG = 6
SLOTS = SUBS + LAG
LAST = 5
CHUNKS = 4


def bit_of(value, index):
    return lax.rem(lax.div(value, jnp.int32(2**index)), jnp.int32(2))


def flip(value, mask, bits):
    total = jnp.int32(0)
    for index in range(bits):
        bit = bit_of(value, index)
        total = total + (1 - bit if mask >> index & 1 else bit) * 2**index
    return total


def dot_nt(left, right):
    return lax.dot_general(left, right, (((1,), (1,)), ((), ())), preferred_element_type=F32)


def split(value):
    high = value.astype(BF16)
    return high, (value - high.astype(F32)).astype(BF16)


def product(left, right):
    (left_high, left_low), (right_high, right_low) = left, right
    return dot_nt(left_high, right_high) + (dot_nt(left_high, right_low) + dot_nt(left_low, right_high))


def kernel(x_hbm, spins_hbm, roster_hbm, out_ref, *scratch):
    (rows, spins_ref, roster_ref, own, stage_x, stage_z, stage_1, got_x, got_z, got_1, sums, mean_ref,
     c_high, c_low, h_high, h_low, b_high, b_low, pay_d, pay_a, pay_b, r0_d, r0_c, r1_d, r1_c,
     r2_d, r2_c, r3_d, r3_c, r4_d, r4_c, cross_7, cross_m, picks,
     load_sem, send_sem, recv_sem) = scratch
    group = lax.axis_index("samp")
    part = lax.axis_index("par")
    core = lax.rem(part, jnp.int32(2))
    zh = lax.rem(lax.div(part, jnp.int32(2)), jnp.int32(4))
    y = lax.div(part, jnp.int32(8))

    def samp_peer(mask):
        return {"samp": flip(group, mask, 3)}

    def par_peer(new_y, new_zh, new_core):
        return {"par": new_y * 8 + new_zh * 2 + new_core}

    sibling = par_peer(y, zh, 1 - core)
    load_spins = pltpu.make_async_copy(spins_hbm, spins_ref, load_sem.at[4])
    load_roster = pltpu.make_async_copy(roster_hbm, roster_ref, load_sem.at[5])
    loads = [
        pltpu.make_async_copy(x_hbm.at[:, :, k % 2, k // 2], rows.at[k], load_sem.at[k]) for k in range(CHUNKS)
    ]
    for load in (load_roster, load_spins, *loads):
        load.start()

    peers = [samp_peer(mask) for mask in range(7, 0, -1)]
    peers += [par_peer(y, flip(zh, mask, 2), core) for mask in (1, 3)]
    peers += [par_peer(flip(y, mask, 2), zh, core) for mask in (1, 3)]
    peers += [sibling]
    barrier = pltpu.get_barrier_semaphore()
    for peer in peers:
        pl.semaphore_signal(barrier, inc=1, device_id=peer, device_id_type=MESH)

    counter = [0]
    open_sends = []

    def fresh():
        counter[0] += 1
        return counter[0] - 1

    def remote(src, dst, peer, index):
        return pltpu.make_async_remote_copy(
            src_ref=src, dst_ref=dst, send_sem=send_sem.at[index], recv_sem=recv_sem.at[index],
            device_id=peer, device_id_type=MESH,
        )

    def start(copy):
        copy.start()
        open_sends.append((None, copy))
        return copy

    def start_under(gate, copy):
        pl.when(gate)(copy.start)
        open_sends.append((gate, copy))
        return copy

    load_roster.wait()
    masks = lax.shift_right_logical(roster_ref[...], 9)
    within = roster_ref[...] & (SG - 1)
    seven_first = masks[0:1] == 7
    other = jnp.where(seven_first, masks[1:2], masks[0:1])
    bits = [bit_of(group, index) for index in range(3)]
    side = jnp.where(other == 4, bits[2], jnp.where((other == 2) | (other == 6), bits[1], bits[0]))
    m_part = jnp.broadcast_to(other, (16, SG))
    z_first = (m_part == 1) | (m_part == 3)

    load_spins.wait()
    site = lax.broadcasted_iota(jnp.int32, (NSITES, SG), 0)
    on_a = lax.rem(lax.div(site, jnp.int32(LSIDE)) + lax.rem(site, jnp.int32(LSIDE)), jnp.int32(2)) == 0
    count = jnp.sum(jnp.where(on_a, spins_ref[...], 0).astype(F32), axis=0, keepdims=True)
    sign_row = 1.0 - 2.0 * (count - 2.0 * jnp.floor(count * 0.5))
    sign = jnp.transpose(jnp.broadcast_to(sign_row, (128, SG)))[:, 0:1].reshape(4, 4, 2, 2, 8, 1)
    side128 = jnp.broadcast_to(side, (128, SG)) == 1
    column_sum = jnp.zeros((8, COLS), F32)
    for k in range(CHUNKS):
        loads[k].wait()
        signed = rows[k] * sign[:, :, k % 2, k // 2]
        rows[k] = signed
        column_sum = column_sum + jnp.sum(signed.reshape(16, 8, COLS), axis=0)
        flat = signed.reshape(128, COLS)
        own[pl.ds(8 * k, 8)] = jnp.where(side128, flat[:, :HALF], flat[:, HALF:]).reshape(8, 16, HALF)
    sums[0] = jnp.sum(column_sum, axis=0, keepdims=True)
    sum_copies = [remote(sums.at[0], sums.at[mask], samp_peer(mask), fresh()) for mask in range(1, 8)]

    hops = {"x": [], "z": [], "1": []}
    hop_masks = {"x": 6, "z": 1, "1": 2}
    hop_sems = {hop: [fresh() for _ in range(2 * (LAST if hop == "1" else LAG))] for hop in hops}

    def send_hop(hop, src, dst):
        sems, copies = hop_sems[hop], hops[hop]
        if len(copies) >= len(sems):
            copies[-len(sems)].wait_send()
        copy = remote(src, dst, samp_peer(hop_masks[hop]), sems[len(copies) % len(sems)])
        copy.start()
        copies.append(copy)

    def exchange(slot):
        before = slot - LAG
        if 0 <= before < SLOTS:
            for hop in "xz":
                hops[hop][before].wait_recv()
        if slot < SLOTS:
            if slot < LAG:
                from_x = from_z = own.at[slot]
            elif slot < SUBS:
                stage_x[slot] = jnp.where(z_first, got_z[before], own[slot])
                stage_z[slot] = jnp.where(z_first, own[slot], got_x[before])
                from_x, from_z = stage_x.at[slot], stage_z.at[slot]
            else:
                from_x, from_z = got_z.at[before], got_x.at[before]
            send_hop("x", from_x, got_x.at[slot])
            send_hop("z", from_z, got_z.at[slot])
        sub = slot - 2 * LAG - LAST
        for sub in range(sub, sub + 1) if slot < SUBS + 2 * LAG else range(sub, SUBS):
            if sub >= 0:
                hops["1"][sub].wait_recv()
        sub = slot - 2 * LAG
        if 0 <= sub < SUBS:
            stage_1[sub] = jnp.where(
                m_part == 2, own[sub],
                jnp.where(m_part == 3, got_z[sub], jnp.where(m_part == 4, got_x[sub], got_z[sub + LAG])),
            )
            send_hop("1", stage_1.at[sub], got_1.at[sub])

    natural = lax.broadcasted_iota(jnp.int32, (1, SG), 1)
    plans = [
        natural,
        jnp.where(seven_first, within[0:1], within[1:2]),
        jnp.where(seven_first, within[1:2], within[0:1]),
    ]

    def place_picks(index):
        plan = plans[index]
        p = plan >> 4
        place = ((plan >> 3) & 1) * 256 + (p & 1) * 128 + (p >> 3) * 32 + ((p >> 1) & 3) * 8 + (plan & 7)
        for first in range(0, SG, 128):
            position = lax.broadcasted_iota(jnp.int32, (128, SG), 0) + first
            picks[index, pl.ds(first, 128)] = jnp.where(position == place, 1.0, 0.0).astype(BF16)

    def centre():
        for copy in sum_copies:
            copy.wait_recv()
        mean = (
            ((sums[0] + sums[1]) + (sums[2] + sums[3])) + ((sums[4] + sums[5]) + (sums[6] + sums[7]))
        ) * (1.0 / SAMPLES)
        mean_ref[...] = jnp.where(side == 1, mean[:, HALF:], mean[:, :HALF])
        for k in range(CHUNKS):
            at = pl.ds(k * 128, 128)
            centred = rows[k].reshape(128, COLS) - mean
            c_high[at], c_low[at] = split(centred)
            h_high[at], h_low[at] = split(jnp.where(side128, centred[:, HALF:], centred[:, :HALF]))

    order_of = ((0, 3, 1, 2), (0, 1, 2, 3))
    hop_pairs = ((1, 3), (3, 1))

    def pair_of(index, q):
        low, high = bit_of(index, 0), bit_of(index, 1)
        return lax.rem(low + high, jnp.int32(2)) if q == 0 else high

    def place_in(index, q):
        return bit_of(index, 1 - q)

    def diagonal(c, half):
        rows_at, at = pl.ds(c * 256, 256), pl.ds(half * 256, 256)
        tile = product((c_high[rows_at], c_low[rows_at]), (c_high[at], c_low[at])).reshape(2, 4, 4, 8, 256)
        for i, to_y in enumerate(order_of[c]):
            for j, to_zh in enumerate(order_of[c]):
                pay_d[:, c, i, j, :, at] = tile[:, to_y, to_zh]

    def gather(k, kind):
        for j in range(8):
            sub = 8 * k + j
            if kind == 0:
                part_rows = jnp.where(z_first, got_x[sub + LAG], got_z[sub + LAG])
            else:
                part_rows = jnp.where(m_part == 1, got_z[sub], jnp.where(m_part == 6, got_x[sub], got_1[sub]))
            at = pl.ds(kind * 128 + 16 * j, 16)
            b_high[at], b_low[at] = split(part_rows - mean_ref[...])

    def tiles(k, kinds):
        at = pl.ds(kinds[0] * 128, len(kinds) * 128)
        tile = product((h_high[...], h_low[...]), (b_high[at], b_low[at]))
        own_tile = tile.reshape(2, 2, 4, 4, 8, len(kinds) * 128)
        back_tile = jnp.transpose(tile).reshape(len(kinds), 4, 4, 8, SG)
        for index, q in enumerate(kinds):
            lanes = slice(index * 128, index * 128 + 128)
            for i, to_y in enumerate(order_of[q]):
                for j, to_zh in enumerate(order_of[q]):
                    pay_b[k, q, i, j] = back_tile[index, to_y, to_zh]
                    for c in range(2):
                        pay_a[k, :, q, i, j, :, pl.ds(c * 128, 128)] = own_tile[c, :, to_y, to_zh, :, lanes]

    def halving(r0, r1, r2, r3, r4, wide, qs=(0, 1)):
        def hop(src, dst, peer):
            index = fresh()
            if wide is None:
                return [(None, start(remote(src, dst, peer, index)))]
            first = pl.ds(0, 256)
            narrow = remote(src.at[..., first], dst.at[..., first], peer, index)
            return [
                (wide[0], start_under(wide[0], remote(src, dst, peer, index))),
                (wide[1], start_under(wide[1], narrow)),
            ]

        def arrive(copies):
            for gate, copy in copies:
                if gate is None:
                    copy.wait_recv()
                else:
                    pl.when(gate)(copy.wait_recv)

        def add(dst, at, other):
            if wide is None:
                dst[at] = dst[at] + other[...]
                return
            first, rest = pl.ds(0, 256), pl.ds(256, SG)
            dst[at + (Ellipsis, first)] = dst[at + (Ellipsis, first)] + other[..., first]

            @pl.when(wide[0])
            def _():
                dst[at + (Ellipsis, rest)] = dst[at + (Ellipsis, rest)] + other[..., rest]

        steps = {}
        for q in qs:
            near = hop_pairs[q][0]
            peer = par_peer(flip(y, near, 2), zh, core)
            steps[q] = hop(r0.at[q, pl.ds(2 * (1 - pair_of(y, q)), 2)], r1.at[q], peer)
        yield
        nexts = {}
        for q in qs:
            far = hop_pairs[q][1]
            pair, place = pair_of(y, q), place_in(y, q)
            arrive(steps[q])
            add(r1, (q, 1 - place), r0.at[q, 2 * pair + 1 - place])
            nexts[q] = hop(r1.at[q, 1 - place], r2.at[q], par_peer(flip(y, far, 2), zh, core))
        for q in qs:
            pair, place = pair_of(y, q), place_in(y, q)
            add(r1, (q, place), r0.at[q, 2 * pair + place])
        yield
        steps = {}
        for q in qs:
            near = hop_pairs[q][0]
            arrive(nexts[q])
            add(r2, (q,), r1.at[q, place_in(y, q)])
            peer = par_peer(y, flip(zh, near, 2), core)
            steps[q] = hop(r2.at[q, pl.ds(2 * (1 - pair_of(zh, q)), 2)], r3.at[q], peer)
        yield
        nexts = {}
        for q in qs:
            far = hop_pairs[q][1]
            pair, place = pair_of(zh, q), place_in(zh, q)
            arrive(steps[q])
            add(r3, (q, 1 - place), r2.at[q, 2 * pair + 1 - place])
            nexts[q] = hop(r3.at[q, 1 - place], r4.at[q], par_peer(y, flip(zh, far, 2), core))
        for q in qs:
            pair, place = pair_of(zh, q), place_in(zh, q)
            add(r3, (q, place), r2.at[q, 2 * pair + place])
        yield
        for q in qs:
            arrive(nexts[q])
            add(r4, (q,), r3.at[q, place_in(zh, q)])

    def reduce_diagonal():
        step = start(remote(pay_d.at[1 - core], r0_d, sibling, fresh()))
        yield
        step.wait_recv()
        r0_d[...] = r0_d[...] + pay_d[core]
        yield from halving(r0_d, r1_d, r2_d, r3_d, r4_d, None)

    cross_sems = [[fresh() for _ in range(7)] for _ in range(2)]

    def reduce_chunk(k, kinds):
        c, to = k // 2, k % 2
        here, there = core == to, core != to
        first, rest = pl.ds(0, 256), pl.ds(256, SG)
        at = pl.ds(kinds[0], len(kinds))
        index = fresh()
        step_a = start_under(here, remote(pay_a.at[k, 1 - core, at], r0_c.at[k, at, ..., first], sibling, index))
        step_b = start_under(there, remote(pay_b.at[k, at], r0_c.at[k, at, ..., rest], sibling, index))
        yield

        @pl.when(there)
        def _():
            step_a.wait_recv()
            r0_c[k, at, ..., first] = r0_c[k, at, ..., first] + pay_a[k, 1 - to, at]

        @pl.when(here)
        def _():
            step_b.wait_recv()
            for q in kinds:
                places = [(order_of[q].index(to_y), order_of[q].index(to_zh)) for to_y in range(4) for to_zh in range(4)]
                for half in range(2):
                    lanes = pl.ds(256 + half * 256 + to * 128, 128)
                    block = jnp.concatenate([r0_c[k, q, i, j, :, lanes] for i, j in places], axis=0)
                    block = jnp.transpose(block).reshape(16, 8, 128)
                    lanes = pl.ds(half * 128, 128)
                    for place, (i, j) in enumerate(places):
                        r0_c[k, q, i, j, :, lanes] = pay_a[k, to, q, i, j, :, lanes] + block[place]
            r0_c[k, at, ..., rest] = r0_c[k, at, ..., rest] + pay_b[k, at]

        yield from halving(r0_c.at[k], r1_c.at[k], r2_c.at[k], r3_c.at[k], r4_c.at[k], (here, there), kinds)
        crossings = []
        for kind in kinds:
            for mask in (7,) if kind == 0 else range(1, 7):
                to_ref = cross_7.at[c] if kind == 0 else cross_m.at[c, mask - 1]
                crossings.append(start_under(
                    here, remote(r4_c.at[k, kind, :, rest], to_ref, samp_peer(mask), cross_sems[c][mask - 1])
                ))
        yield

        @pl.when(here)
        def _():
            for copy in crossings:
                copy.wait_recv()

    def ordered(value, index):
        value = value * (1.0 / SAMPLES)
        high, low = split(value)
        rest = value - high.astype(F32) - low.astype(F32)
        stacked = jnp.concatenate([high, low, rest.astype(BF16)], axis=0)
        moved = lax.dot_general(stacked, picks[index], (((1,), (0,)), ((), ())), preferred_element_type=F32)
        return moved[0:16] + (moved[16:32] + moved[32:48])

    def whole(kind):
        blocks = []
        for c in range(2):
            own_part = jnp.concatenate([r4_c[k, kind, :, pl.ds(c * 128, 128)] for k in range(CHUNKS)], axis=1)
            if kind == 0:
                arrived = cross_7[c]
            else:
                arrived = cross_m[c, 0]
                for mask in range(2, 7):
                    arrived = jnp.where(other == mask, cross_m[c, mask - 1], arrived)
            blocks.append(own_part + arrived)
        return jnp.concatenate(blocks, axis=0)

    def scope(name):
        return jax.named_scope(name)

    walks = {}

    def advance(name):
        next(walks[name], None)

    def begin(name, walk):
        walks[name] = walk
        advance(name)

    def make_d(index):
        diagonal(index // 2, index % 2)
        if index == 3:
            begin("d", reduce_diagonal())

    both = (0, 1)

    def make(k, kinds):
        for kind in kinds:
            gather(k, kind)
        tiles(k, kinds)
        begin((k, kinds), reduce_chunk(k, kinds))

    with scope("bar"):
        pl.semaphore_wait(barrier, len(peers))
    for copy in sum_copies:
        start(copy)
    c0, c1, c2, c3 = ((k, both) for k in range(4))
    after = {
        0: [(place_picks, 0)],
        1: [(place_picks, 1)],
        2: [(place_picks, 2)],
        7: [(centre,)],
        9: [(make_d, 0)],
        11: [(make_d, 1)],
        13: [(make_d, 2)],
        15: [(make_d, 3)],
        22: [(advance, "d")],
        24: [(make, 0, both)],
        29: [(advance, "d")],
        31: [(advance, c0)],
        32: [(make, 1, both)],
        38: [(advance, c0)],
        39: [(advance, c1)],
        40: [(make, 2, both), (advance, "d")],
        43: [(advance, c0), (advance, c2)],
        44: [(make, 3, both)],
    }
    for slot in range(SUBS + 2 * LAG + 1):
        with scope(f"ex{slot}"):
            exchange(slot)
        for job, *about in after.get(slot, []):
            with scope(f"job{slot}_{job.__name__}_{about}"):
                job(*about)
    def finish_d():
        tile_d = jnp.concatenate([r4_d[0], r4_d[1]], axis=0)
        out_ref[0, 0] = ordered(tile_d, 0)
        return tile_d
    for turn, name in enumerate((c1, c3, "d", c0, c2, c3, c1, "d", "tile", c2, c3, c0, c1, c2, c3, c1, c2, c3, c0, c1, c2, c3)):
        with scope(f"tail{turn}_{name}"):
            if name == "tile":
                tile_d = finish_d()
            else:
                advance(name)
    with scope("final"):
        tile_7 = ordered(whole(0), 1)
        tile_m = ordered(jnp.where(other == 0, tile_d, whole(1)), 2)
        out_ref[0, 1] = jnp.where(seven_first, tile_7, tile_m)
        out_ref[0, 2] = jnp.where(seven_first, tile_m, tile_7)
    with scope("drain"):
        for hop, copies in hops.items():
            for copy in copies[-len(hop_sems[hop]):]:
                copy.wait_send()
        for gate, copy in open_sends:
            if gate is None:
                copy.wait_send()
            else:
                pl.when(gate)(copy.wait_send)


def gram(x, spins, roster):
    vmem = pltpu.VMEM

    def halves(lead, width):
        return [
            vmem(lead + (2, 4, 4, 8, width), F32),
            vmem(lead + (2, 2, 4, 8, width), F32),
            vmem(lead + (2, 4, 8, width), F32),
            vmem(lead + (2, 2, 8, width), F32),
            vmem(lead + (2, 8, width), F32),
        ]

    sets = [halves((), SG), halves((CHUNKS,), 256 + SG)]
    scratch = [
        vmem((CHUNKS, 4, 4, 8, COLS), F32),
        vmem((NSITES, SG), jnp.int32),
        vmem((2, SG), jnp.int32),
        vmem((SUBS, 16, HALF), F32),
        vmem((SLOTS, 16, HALF), F32),
        vmem((SLOTS, 16, HALF), F32),
        vmem((SUBS, 16, HALF), F32),
        vmem((SLOTS, 16, HALF), F32),
        vmem((SLOTS, 16, HALF), F32),
        vmem((SUBS, 16, HALF), F32),
        vmem((8, 1, COLS), F32),
        vmem((1, HALF), F32),
        vmem((SG, COLS), BF16),
        vmem((SG, COLS), BF16),
        vmem((SG, HALF), BF16),
        vmem((SG, HALF), BF16),
        vmem((256, HALF), BF16),
        vmem((256, HALF), BF16),
        vmem((2, 2, 4, 4, 8, SG), F32),
        vmem((CHUNKS, 2, 2, 4, 4, 8, 256), F32),
        vmem((CHUNKS, 2, 4, 4, 8, SG), F32),
        *[one[step] for step in range(5) for one in sets],
        vmem((2, 8, SG), F32),
        vmem((2, 6, 8, SG), F32),
        vmem((3, SG, SG), BF16),
        pltpu.SemaphoreType.DMA((6,)),
        pltpu.SemaphoreType.DMA((100,)),
        pltpu.SemaphoreType.DMA((100,)),
    ]
    return pl.pallas_call(
        kernel,
        out_shape=jax.ShapeDtypeStruct((1, 3, 16, SG), F32),
        in_specs=[pl.BlockSpec(memory_space=pltpu.HBM)] * 3,
        out_specs=pl.BlockSpec(memory_space=pltpu.VMEM),
        scratch_shapes=scratch,
        compiler_params=pltpu.CompilerParams(
            collective_id=0, has_side_effects=True, vmem_limit_bytes=55040 * 1024
        ),
        name="gram",
    )(x, spins, roster)


def on_device(log_derivs, spins, roster):
    return gram(log_derivs.reshape(4, 4, 2, 2, 8, COLS), spins.T, roster)


def solution(mesh):
    in_specs = (P("samp", "par"), P("samp", None), P())
    out_specs = P("samp", None, "par", None)
    return jax.shard_map(
        on_device, mesh=mesh, in_specs=in_specs, out_specs=out_specs, check_vma=False
    )
```

```python
import functools

import jax
import jax.numpy as jnp
from jax import lax
from jax.experimental import pallas as pl
from jax.experimental.pallas import tpu as pltpu
from jax.sharding import PartitionSpec as P

MESH = pl.DeviceIdType.MESH
F32, BF16 = jnp.float32, jnp.bfloat16

SG = 512
NSITES = 100
LSIDE = 10
COLS = 1024
HALF = COLS // 2
SAMPLES = 4096
SUBS = 32
LAG = 7
SLOTS = SUBS + LAG
SENDS = 24
LAST = 5
CHUNKS = 4


def bit_of(value, index):
    return lax.rem(lax.div(value, jnp.int32(2**index)), jnp.int32(2))


def flip(value, mask, bits):
    total = jnp.int32(0)
    for index in range(bits):
        bit = bit_of(value, index)
        total = total + (1 - bit if mask >> index & 1 else bit) * 2**index
    return total


def dot_nt(left, right):
    return lax.dot_general(left, right, (((1,), (1,)), ((), ())), preferred_element_type=F32)


def split(value):
    high = value.astype(BF16)
    return high, (value - high.astype(F32)).astype(BF16)


def product(left, right):
    (left_high, left_low), (right_high, right_low) = left, right
    return dot_nt(left_high, right_high) + (dot_nt(left_high, right_low) + dot_nt(left_low, right_high))


def kernel(x_hbm, spins_hbm, roster_hbm, out_ref, *scratch):
    (rows, spins_ref, roster_ref, own, stage_x, stage_z, stage_1, got_x, got_z, got_1, sums, mean_ref,
     c_high, c_low, h_high, h_low, b_high, b_low, pay_d, pay_a, pay_b, r0_d, r0_c, r1_d, r1_c,
     r2_d, r2_c, r3_d, r3_c, r4_d, r4_c, cross_7, cross_m, picks,
     load_sem, send_sem, recv_sem) = scratch
    group = lax.axis_index("samp")
    part = lax.axis_index("par")
    core = lax.rem(part, jnp.int32(2))
    zh = lax.rem(lax.div(part, jnp.int32(2)), jnp.int32(4))
    y = lax.div(part, jnp.int32(8))

    def samp_peer(mask):
        return {"samp": flip(group, mask, 3)}

    def par_peer(new_y, new_zh, new_core):
        return {"par": new_y * 8 + new_zh * 2 + new_core}

    sibling = par_peer(y, zh, 1 - core)
    load_spins = pltpu.make_async_copy(spins_hbm, spins_ref, load_sem.at[4])
    load_roster = pltpu.make_async_copy(roster_hbm, roster_ref, load_sem.at[5])
    loads = [
        pltpu.make_async_copy(x_hbm.at[:, :, k % 2, k // 2], rows.at[k], load_sem.at[k]) for k in range(CHUNKS)
    ]
    for load in (load_roster, load_spins, *loads):
        load.start()

    peers = [samp_peer(mask) for mask in range(7, 0, -1)]
    peers += [par_peer(y, flip(zh, mask, 2), core) for mask in (1, 3)]
    peers += [par_peer(flip(y, mask, 2), zh, core) for mask in (1, 3)]
    peers += [sibling]
    barrier = pltpu.get_barrier_semaphore()
    for peer in peers:
        pl.semaphore_signal(barrier, inc=1, device_id=peer, device_id_type=MESH)

    def scope(name):
        return jax.named_scope(name)

    counter = [0]
    turn_of_send = [0]
    open_sends = [[] for _ in range(SENDS)]

    def fresh():
        counter[0] += 1
        return counter[0] - 1

    def remote(src, dst, peer, index, send_index):
        return pltpu.make_async_remote_copy(
            src_ref=src, dst_ref=dst, send_sem=send_sem.at[send_index], recv_sem=recv_sem.at[index],
            device_id=peer, device_id_type=MESH,
        )

    def wait_sends(slot):
        for gate, copy in open_sends[slot]:
            if gate is None:
                copy.wait_send()
            else:
                pl.when(gate)(copy.wait_send)
        open_sends[slot] = []

    def start(choices, peer, index):
        slot = turn_of_send[0] % SENDS
        turn_of_send[0] += 1
        wait_sends(slot)
        copies = []
        for gate, src, dst in choices:
            copy = remote(src, dst, peer, index, slot)
            if gate is None:
                copy.start()
            else:
                pl.when(gate)(copy.start)
            copies.append((gate, copy))
        open_sends[slot] = copies
        return copies

    load_roster.wait()
    masks = lax.shift_right_logical(roster_ref[...], 9)
    within = roster_ref[...] & (SG - 1)
    seven_first = masks[0:1] == 7
    other = jnp.where(seven_first, masks[1:2], masks[0:1])
    bits = [bit_of(group, index) for index in range(3)]
    side = jnp.where(other == 4, bits[2], jnp.where((other == 2) | (other == 6), bits[1], bits[0]))
    m_part = jnp.broadcast_to(other, (16, SG))
    z_first = (m_part == 1) | (m_part == 3)

    load_spins.wait()
    site = lax.broadcasted_iota(jnp.int32, (NSITES, SG), 0)
    on_a = lax.rem(lax.div(site, jnp.int32(LSIDE)) + lax.rem(site, jnp.int32(LSIDE)), jnp.int32(2)) == 0
    count = jnp.sum(jnp.where(on_a, spins_ref[...], 0).astype(F32), axis=0, keepdims=True)
    sign_row = 1.0 - 2.0 * (count - 2.0 * jnp.floor(count * 0.5))
    sign = jnp.transpose(jnp.broadcast_to(sign_row, (128, SG)))[:, 0:1].reshape(4, 4, 2, 2, 8, 1)
    side128 = jnp.broadcast_to(side, (128, SG)) == 1
    hops = {"x": [], "z": [], "1": []}
    hop_masks = {"x": 6, "z": 1, "1": 2}
    hop_sems = {hop: [fresh() for _ in range(2 * (LAST if hop == "1" else LAG))] for hop in hops}
    hop_sends = {hop: [SENDS + index for index in sems] for hop, sems in hop_sems.items()}

    def send_hop(hop, src, dst):
        sems, copies = hop_sems[hop], hops[hop]
        if len(copies) >= len(sems):
            copies[-len(sems)].wait_send()
        turn = len(copies) % len(sems)
        copy = remote(src, dst, samp_peer(hop_masks[hop]), sems[turn], hop_sends[hop][turn])
        copy.start()
        copies.append(copy)

    def exchange(slot):
        before = slot - LAG
        if 0 <= before < SLOTS:
            for hop in "xz":
                hops[hop][before].wait_recv()
        if slot < SLOTS:
            if slot < LAG:
                from_x = from_z = own.at[slot]
            elif slot < SUBS:
                stage_x[slot] = jnp.where(z_first, got_z[before], own[slot])
                stage_z[slot] = jnp.where(z_first, own[slot], got_x[before])
                from_x, from_z = stage_x.at[slot], stage_z.at[slot]
            else:
                from_x, from_z = got_z.at[before], got_x.at[before]
            send_hop("x", from_x, got_x.at[slot])
            send_hop("z", from_z, got_z.at[slot])
        sub = slot - 2 * LAG - LAST
        for sub in range(sub, sub + 1) if slot < SUBS + 2 * LAG else range(sub, SUBS):
            if sub >= 0:
                hops["1"][sub].wait_recv()
        sub = slot - 2 * LAG
        if 0 <= sub < SUBS:
            stage_1[sub] = jnp.where(
                m_part == 2, own[sub],
                jnp.where(m_part == 3, got_z[sub], jnp.where(m_part == 4, got_x[sub], got_z[sub + LAG])),
            )
            send_hop("1", stage_1.at[sub], got_1.at[sub])

    column_sum = jnp.zeros((8, COLS), F32)
    for k in range(CHUNKS):
        loads[k].wait()
        signed = rows[k] * sign[:, :, k % 2, k // 2]
        rows[k] = signed
        column_sum = column_sum + jnp.sum(signed.reshape(16, 8, COLS), axis=0)
        flat = signed.reshape(128, COLS)
        own[pl.ds(8 * k, 8)] = jnp.where(side128, flat[:, :HALF], flat[:, HALF:]).reshape(8, 16, HALF)
    sums[0] = jnp.sum(column_sum, axis=0, keepdims=True)
    with scope("bar"):
        pl.semaphore_wait(barrier, len(peers))
    sum_copies = []
    for mask in range(1, 8):
        sum_copies += start([(None, sums.at[0], sums.at[mask])], samp_peer(mask), fresh())

    natural = lax.broadcasted_iota(jnp.int32, (1, SG), 1)
    plans = [
        natural,
        jnp.where(seven_first, within[0:1], within[1:2]),
        jnp.where(seven_first, within[1:2], within[0:1]),
    ]

    def place_picks(index):
        plan = plans[index]
        p = plan >> 4
        place = ((plan >> 3) & 1) * 256 + (p & 1) * 128 + (p >> 3) * 32 + ((p >> 1) & 3) * 8 + (plan & 7)
        for first in range(0, SG, 128):
            position = lax.broadcasted_iota(jnp.int32, (128, SG), 0) + first
            picks[index, pl.ds(first, 128)] = jnp.where(position == place, 1.0, 0.0).astype(BF16)

    def centre():
        for _, copy in sum_copies:
            copy.wait_recv()
        mean = (
            ((sums[0] + sums[1]) + (sums[2] + sums[3])) + ((sums[4] + sums[5]) + (sums[6] + sums[7]))
        ) * (1.0 / SAMPLES)
        mean_ref[...] = jnp.where(side == 1, mean[:, HALF:], mean[:, :HALF])
        for k in range(CHUNKS):
            at = pl.ds(k * 128, 128)
            centred = rows[k].reshape(128, COLS) - mean
            c_high[at], c_low[at] = split(centred)
            h_high[at], h_low[at] = split(jnp.where(side128, centred[:, HALF:], centred[:, :HALF]))

    order_of = ((0, 3, 1, 2), (0, 1, 2, 3))
    hop_pairs = ((1, 3), (3, 1))

    def pair_of(index, q):
        low, high = bit_of(index, 0), bit_of(index, 1)
        return lax.rem(low + high, jnp.int32(2)) if q == 0 else high

    def place_in(index, q):
        return bit_of(index, 1 - q)

    def diagonal(c, half):
        rows_at, at = pl.ds(c * 256, 256), pl.ds(half * 256, 256)
        tile = product((c_high[rows_at], c_low[rows_at]), (c_high[at], c_low[at])).reshape(2, 4, 4, 8, 256)
        for i, to_y in enumerate(order_of[c]):
            for j, to_zh in enumerate(order_of[c]):
                pay_d[:, c, i, j, :, at] = tile[:, to_y, to_zh]

    def gather(k, kind):
        for j in range(8):
            sub = 8 * k + j
            if kind == 0:
                part_rows = jnp.where(z_first, got_x[sub + LAG], got_z[sub + LAG])
            else:
                part_rows = jnp.where(m_part == 1, got_z[sub], jnp.where(m_part == 6, got_x[sub], got_1[sub]))
            at = pl.ds(kind * 128 + 16 * j, 16)
            b_high[at], b_low[at] = split(part_rows - mean_ref[...])

    def tiles(k, kinds):
        at = pl.ds(kinds[0] * 128, len(kinds) * 128)
        tile = product((h_high[...], h_low[...]), (b_high[at], b_low[at]))
        own_tile = tile.reshape(2, 2, 4, 4, 8, len(kinds) * 128)
        back_tile = jnp.transpose(tile).reshape(len(kinds), 4, 4, 8, SG)
        for index, q in enumerate(kinds):
            lanes = slice(index * 128, index * 128 + 128)
            for i, to_y in enumerate(order_of[q]):
                for j, to_zh in enumerate(order_of[q]):
                    pay_b[k, q, i, j] = back_tile[index, to_y, to_zh]
                    for c in range(2):
                        pay_a[k, :, q, i, j, :, pl.ds(c * 128, 128)] = own_tile[c, :, to_y, to_zh, :, lanes]

    def halving(r0, r1, r2, r3, r4, wide, qs=(0, 1)):
        def hop(src, dst, peer):
            if wide is None:
                return start([(None, src, dst)], peer, fresh())
            first = pl.ds(0, 256)
            return start([(wide[0], src, dst), (wide[1], src.at[..., first], dst.at[..., first])], peer, fresh())

        def arrive(copies):
            for gate, copy in copies:
                if gate is None:
                    copy.wait_recv()
                else:
                    pl.when(gate)(copy.wait_recv)

        def add(dst, at, other):
            if wide is None:
                dst[at] = dst[at] + other[...]
                return
            first, rest = pl.ds(0, 256), pl.ds(256, SG)
            dst[at + (Ellipsis, first)] = dst[at + (Ellipsis, first)] + other[..., first]

            @pl.when(wide[0])
            def _():
                dst[at + (Ellipsis, rest)] = dst[at + (Ellipsis, rest)] + other[..., rest]

        steps = {}
        for q in qs:
            near = hop_pairs[q][0]
            peer = par_peer(flip(y, near, 2), zh, core)
            steps[q] = hop(r0.at[q, pl.ds(2 * (1 - pair_of(y, q)), 2)], r1.at[q], peer)
        yield
        nexts = {}
        for q in qs:
            far = hop_pairs[q][1]
            pair, place = pair_of(y, q), place_in(y, q)
            arrive(steps[q])
            add(r1, (q, 1 - place), r0.at[q, 2 * pair + 1 - place])
            nexts[q] = hop(r1.at[q, 1 - place], r2.at[q], par_peer(flip(y, far, 2), zh, core))
        for q in qs:
            pair, place = pair_of(y, q), place_in(y, q)
            add(r1, (q, place), r0.at[q, 2 * pair + place])
        yield
        steps = {}
        for q in qs:
            near = hop_pairs[q][0]
            arrive(nexts[q])
            add(r2, (q,), r1.at[q, place_in(y, q)])
            peer = par_peer(y, flip(zh, near, 2), core)
            steps[q] = hop(r2.at[q, pl.ds(2 * (1 - pair_of(zh, q)), 2)], r3.at[q], peer)
        yield
        nexts = {}
        for q in qs:
            far = hop_pairs[q][1]
            pair, place = pair_of(zh, q), place_in(zh, q)
            arrive(steps[q])
            add(r3, (q, 1 - place), r2.at[q, 2 * pair + 1 - place])
            nexts[q] = hop(r3.at[q, 1 - place], r4.at[q], par_peer(y, flip(zh, far, 2), core))
        for q in qs:
            pair, place = pair_of(zh, q), place_in(zh, q)
            add(r3, (q, place), r2.at[q, 2 * pair + place])
        yield
        for q in qs:
            arrive(nexts[q])
            add(r4, (q,), r3.at[q, place_in(zh, q)])

    def reduce_diagonal():
        ((_, step),) = start([(None, pay_d.at[1 - core], r0_d)], sibling, fresh())
        yield
        step.wait_recv()
        r0_d[...] = r0_d[...] + pay_d[core]
        yield from halving(r0_d, r1_d, r2_d, r3_d, r4_d, None)

    cross_sems = [[fresh() for _ in range(7)] for _ in range(2)]

    def reduce_chunk(k, kinds):
        c, to = k // 2, k % 2
        here, there = core == to, core != to
        first, rest = pl.ds(0, 256), pl.ds(256, SG)
        at = pl.ds(kinds[0], len(kinds))
        (_, step_a), (_, step_b) = start(
            [
                (here, pay_a.at[k, 1 - core, at], r0_c.at[k, at, ..., first]),
                (there, pay_b.at[k, at], r0_c.at[k, at, ..., rest]),
            ],
            sibling,
            fresh(),
        )
        yield

        @pl.when(there)
        def _():
            step_a.wait_recv()
            r0_c[k, at, ..., first] = r0_c[k, at, ..., first] + pay_a[k, 1 - to, at]

        @pl.when(here)
        def _():
            step_b.wait_recv()
            for q in kinds:
                places = [(order_of[q].index(to_y), order_of[q].index(to_zh)) for to_y in range(4) for to_zh in range(4)]
                for half in range(2):
                    lanes = pl.ds(256 + half * 256 + to * 128, 128)
                    block = jnp.concatenate([r0_c[k, q, i, j, :, lanes] for i, j in places], axis=0)
                    block = jnp.transpose(block).reshape(16, 8, 128)
                    lanes = pl.ds(half * 128, 128)
                    for place, (i, j) in enumerate(places):
                        r0_c[k, q, i, j, :, lanes] = pay_a[k, to, q, i, j, :, lanes] + block[place]
            r0_c[k, at, ..., rest] = r0_c[k, at, ..., rest] + pay_b[k, at]

        yield from halving(r0_c.at[k], r1_c.at[k], r2_c.at[k], r3_c.at[k], r4_c.at[k], (here, there), kinds)
        crossings = []
        for kind in kinds:
            for mask in (7,) if kind == 0 else range(1, 7):
                to_ref = cross_7.at[c] if kind == 0 else cross_m.at[c, mask - 1]
                ((_, copy),) = start(
                    [(here, r4_c.at[k, kind, :, rest], to_ref)], samp_peer(mask), cross_sems[c][mask - 1]
                )
                crossings.append(copy)
        yield

        @pl.when(here)
        def _():
            for copy in crossings:
                copy.wait_recv()

    def ordered(value, index):
        value = value * (1.0 / SAMPLES)
        high, low = split(value)
        rest = value - high.astype(F32) - low.astype(F32)
        stacked = jnp.concatenate([high, low, rest.astype(BF16)], axis=0)
        moved = lax.dot_general(stacked, picks[index], (((1,), (0,)), ((), ())), preferred_element_type=F32)
        return moved[0:16] + (moved[16:32] + moved[32:48])

    def whole(kind):
        blocks = []
        for c in range(2):
            own_part = jnp.concatenate([r4_c[k, kind, :, pl.ds(c * 128, 128)] for k in range(CHUNKS)], axis=1)
            if kind == 0:
                arrived = cross_7[c]
            else:
                arrived = cross_m[c, 0]
                for mask in range(2, 7):
                    arrived = jnp.where(other == mask, cross_m[c, mask - 1], arrived)
            blocks.append(own_part + arrived)
        return jnp.concatenate(blocks, axis=0)

    walks = {}

    def advance(name):
        next(walks[name], None)

    def begin(name, walk):
        walks[name] = walk
        advance(name)

    def make_d(index):
        diagonal(index // 2, index % 2)
        if index == 3:
            begin("d", reduce_diagonal())

    both = (0, 1)

    def make(k, kinds):
        for kind in kinds:
            gather(k, kind)
        tiles(k, kinds)
        begin((k, kinds), reduce_chunk(k, kinds))

    c0, c1, c2, c3 = ((k, both) for k in range(4))
    after = {
        0: [(place_picks, 0)],
        1: [(place_picks, 1)],
        2: [(place_picks, 2)],
        7: [(centre,)],
        9: [(make_d, 0)],
        11: [(make_d, 1)],
        13: [(make_d, 2)],
        15: [(make_d, 3)],
        24: [(advance, "d")],
        26: [(make, 0, both)],
        31: [(advance, "d")],
        33: [(advance, c0)],
        34: [(make, 1, both)],
        40: [(advance, c0)],
        41: [(advance, c1)],
        42: [(make, 2, both), (advance, "d")],
        45: [(advance, c0), (advance, c2)],
        46: [(make, 3, both)],
    }
    for slot in range(SUBS + 2 * LAG + 1):
        with scope(f"ex{slot}"):
            exchange(slot)
        for job, *about in after.get(slot, []):
            with scope(f"job{slot}_{job.__name__}_{about}"):
                job(*about)
    def finish_d():
        tile_d = jnp.concatenate([r4_d[0], r4_d[1]], axis=0)
        out_ref[0, 0] = ordered(tile_d, 0)
        return tile_d
    for turn, name in enumerate((c1, c3, "d", c0, c2, c3, c1, "d", "tile", c2, c3, c0, c1, c2, c3, c1, c2, c3, c0, c1, c2, c3)):
        with scope(f"tail{turn}_{name}"):
            if name == "tile":
                tile_d = finish_d()
            else:
                advance(name)
    with scope("final"):
        tile_7 = ordered(whole(0), 1)
        tile_m = ordered(jnp.where(other == 0, tile_d, whole(1)), 2)
        out_ref[0, 1] = jnp.where(seven_first, tile_7, tile_m)
        out_ref[0, 2] = jnp.where(seven_first, tile_m, tile_7)
    with scope("drain"):
        for hop, copies in hops.items():
            for copy in copies[-len(hop_sems[hop]):]:
                copy.wait_send()
        for slot in range(SENDS):
            wait_sends(slot)


def gram(x, spins, roster):
    vmem = pltpu.VMEM

    def halves(lead, width):
        return [
            vmem(lead + (2, 4, 4, 8, width), F32),
            vmem(lead + (2, 2, 4, 8, width), F32),
            vmem(lead + (2, 4, 8, width), F32),
            vmem(lead + (2, 2, 8, width), F32),
            vmem(lead + (2, 8, width), F32),
        ]

    sets = [halves((), SG), halves((CHUNKS,), 256 + SG)]
    scratch = [
        vmem((CHUNKS, 4, 4, 8, COLS), F32),
        vmem((NSITES, SG), jnp.int32),
        vmem((2, SG), jnp.int32),
        vmem((SUBS, 16, HALF), F32),
        vmem((SLOTS, 16, HALF), F32),
        vmem((SLOTS, 16, HALF), F32),
        vmem((SUBS, 16, HALF), F32),
        vmem((SLOTS, 16, HALF), F32),
        vmem((SLOTS, 16, HALF), F32),
        vmem((SUBS, 16, HALF), F32),
        vmem((8, 1, COLS), F32),
        vmem((1, HALF), F32),
        vmem((SG, COLS), BF16),
        vmem((SG, COLS), BF16),
        vmem((SG, HALF), BF16),
        vmem((SG, HALF), BF16),
        vmem((256, HALF), BF16),
        vmem((256, HALF), BF16),
        vmem((2, 2, 4, 4, 8, SG), F32),
        vmem((CHUNKS, 2, 2, 4, 4, 8, 256), F32),
        vmem((CHUNKS, 2, 4, 4, 8, SG), F32),
        *[one[step] for step in range(5) for one in sets],
        vmem((2, 8, SG), F32),
        vmem((2, 6, 8, SG), F32),
        vmem((3, SG, SG), BF16),
        pltpu.SemaphoreType.DMA((6,)),
        pltpu.SemaphoreType.DMA((SENDS + 4 * LAG + 2 * LAST,)),
        pltpu.SemaphoreType.DMA((104,)),
    ]
    return pl.pallas_call(
        kernel,
        out_shape=jax.ShapeDtypeStruct((1, 3, 16, SG), F32),
        in_specs=[pl.BlockSpec(memory_space=pltpu.HBM)] * 3,
        out_specs=pl.BlockSpec(memory_space=pltpu.VMEM),
        scratch_shapes=scratch,
        compiler_params=pltpu.CompilerParams(
            collective_id=0, has_side_effects=True, vmem_limit_bytes=55040 * 1024
        ),
        name="gram",
    )(x, spins, roster)


def on_device(log_derivs, spins, roster):
    return gram(log_derivs.reshape(4, 4, 2, 2, 8, COLS), spins.T, roster)


def solution(mesh):
    in_specs = (P("samp", "par"), P("samp", None), P())
    out_specs = P("samp", None, "par", None)
    return jax.shard_map(
        on_device, mesh=mesh, in_specs=in_specs, out_specs=out_specs, check_vma=False
    )
```

```python
import functools

import jax
import jax.numpy as jnp
from jax import lax
from jax.experimental import pallas as pl
from jax.experimental.pallas import tpu as pltpu
from jax.sharding import PartitionSpec as P

MESH = pl.DeviceIdType.MESH
F32, BF16 = jnp.float32, jnp.bfloat16

SG = 512
NSITES = 100
LSIDE = 10
COLS = 1024
HALF = COLS // 2
SAMPLES = 4096
SUBS = 32
LAG = 7
SLOTS = SUBS + LAG
SENDS = 24
LAST = 5
CHUNKS = 4


def bit_of(value, index):
    return lax.rem(lax.div(value, jnp.int32(2**index)), jnp.int32(2))


def flip(value, mask, bits):
    total = jnp.int32(0)
    for index in range(bits):
        bit = bit_of(value, index)
        total = total + (1 - bit if mask >> index & 1 else bit) * 2**index
    return total


def dot_nt(left, right):
    return lax.dot_general(left, right, (((1,), (1,)), ((), ())), preferred_element_type=F32)


def split(value):
    high = value.astype(BF16)
    return high, (value - high.astype(F32)).astype(BF16)


def product(left, right):
    (left_high, left_low), (right_high, right_low) = left, right
    return dot_nt(left_high, right_high) + (dot_nt(left_high, right_low) + dot_nt(left_low, right_high))


def kernel(x_hbm, spins_hbm, roster_hbm, out_ref, *scratch):
    (rows, spins_ref, roster_ref, own, stage_x, stage_z, stage_1, got_x, got_z, got_1, sums, mean_ref,
     c_high, c_low, h_high, h_low, b_high, b_low, pay_d, pay_a, pay_b, r0_d, r0_c, r1_d, r1_c,
     r2_d, r2_c, r3_d, r3_c, r4_d, r4_c, cross_7, cross_m, picks,
     load_sem, send_sem, recv_sem) = scratch
    group = lax.axis_index("samp")
    part = lax.axis_index("par")
    core = lax.rem(part, jnp.int32(2))
    zh = lax.rem(lax.div(part, jnp.int32(2)), jnp.int32(4))
    y = lax.div(part, jnp.int32(8))

    def samp_peer(mask):
        return {"samp": flip(group, mask, 3)}

    def par_peer(new_y, new_zh, new_core):
        return {"par": new_y * 8 + new_zh * 2 + new_core}

    sibling = par_peer(y, zh, 1 - core)
    load_spins = pltpu.make_async_copy(spins_hbm, spins_ref, load_sem.at[4])
    load_roster = pltpu.make_async_copy(roster_hbm, roster_ref, load_sem.at[5])
    loads = [
        pltpu.make_async_copy(x_hbm.at[:, :, k % 2, k // 2], rows.at[k], load_sem.at[k]) for k in range(CHUNKS)
    ]
    for load in (load_roster, load_spins, *loads):
        load.start()

    peers = [samp_peer(mask) for mask in range(7, 0, -1)]
    peers += [par_peer(y, flip(zh, mask, 2), core) for mask in (1, 3)]
    peers += [par_peer(flip(y, mask, 2), zh, core) for mask in (1, 3)]
    peers += [sibling]
    barrier = pltpu.get_barrier_semaphore()
    for peer in peers:
        pl.semaphore_signal(barrier, inc=1, device_id=peer, device_id_type=MESH)

    def scope(name):
        return jax.named_scope(name)

    counter = [0]
    turn_of_send = [0]
    open_sends = [[] for _ in range(SENDS)]

    def fresh():
        counter[0] += 1
        return counter[0] - 1

    def remote(src, dst, peer, index, send_index):
        return pltpu.make_async_remote_copy(
            src_ref=src, dst_ref=dst, send_sem=send_sem.at[send_index], recv_sem=recv_sem.at[index],
            device_id=peer, device_id_type=MESH,
        )

    def wait_sends(slot):
        for gate, copy in open_sends[slot]:
            if gate is None:
                copy.wait_send()
            else:
                pl.when(gate)(copy.wait_send)
        open_sends[slot] = []

    def start(choices, peer, index):
        slot = turn_of_send[0] % SENDS
        turn_of_send[0] += 1
        wait_sends(slot)
        copies = []
        for gate, src, dst in choices:
            copy = remote(src, dst, peer, index, slot)
            if gate is None:
                copy.start()
            else:
                pl.when(gate)(copy.start)
            copies.append((gate, copy))
        open_sends[slot] = copies
        return copies

    load_roster.wait()
    masks = lax.shift_right_logical(roster_ref[...], 9)
    within = roster_ref[...] & (SG - 1)
    seven_first = masks[0:1] == 7
    other = jnp.where(seven_first, masks[1:2], masks[0:1])
    bits = [bit_of(group, index) for index in range(3)]
    side = jnp.where(other == 4, bits[2], jnp.where((other == 2) | (other == 6), bits[1], bits[0]))
    m_part = jnp.broadcast_to(other, (16, SG))
    z_first = (m_part == 1) | (m_part == 3)

    load_spins.wait()
    site = lax.broadcasted_iota(jnp.int32, (NSITES, SG), 0)
    on_a = lax.rem(lax.div(site, jnp.int32(LSIDE)) + lax.rem(site, jnp.int32(LSIDE)), jnp.int32(2)) == 0
    count = jnp.sum(jnp.where(on_a, spins_ref[...], 0).astype(F32), axis=0, keepdims=True)
    sign_row = 1.0 - 2.0 * (count - 2.0 * jnp.floor(count * 0.5))
    sign = jnp.transpose(jnp.broadcast_to(sign_row, (128, SG)))[:, 0:1].reshape(4, 4, 2, 2, 8, 1)
    side128 = jnp.broadcast_to(side, (128, SG)) == 1
    hops = {"x": [], "z": [], "1": []}
    hop_masks = {"x": 6, "z": 1, "1": 2}
    hop_sems = {hop: [fresh() for _ in range(2 * (LAST if hop == "1" else LAG))] for hop in hops}
    hop_sends = {hop: [SENDS + index for index in sems] for hop, sems in hop_sems.items()}

    def send_hop(hop, src, dst):
        sems, copies = hop_sems[hop], hops[hop]
        if len(copies) >= len(sems):
            copies[-len(sems)].wait_send()
        turn = len(copies) % len(sems)
        copy = remote(src, dst, samp_peer(hop_masks[hop]), sems[turn], hop_sends[hop][turn])
        copy.start()
        copies.append(copy)

    def exchange(slot):
        before = slot - LAG
        if 0 <= before < SLOTS:
            for hop in "xz":
                hops[hop][before].wait_recv()
        if slot < SLOTS:
            if slot < LAG:
                from_x = from_z = own.at[slot]
            elif slot < SUBS:
                stage_x[slot] = jnp.where(z_first, got_z[before], own[slot])
                stage_z[slot] = jnp.where(z_first, own[slot], got_x[before])
                from_x, from_z = stage_x.at[slot], stage_z.at[slot]
            else:
                from_x, from_z = got_z.at[before], got_x.at[before]
            send_hop("x", from_x, got_x.at[slot])
            send_hop("z", from_z, got_z.at[slot])
        sub = slot - 2 * LAG - LAST
        for sub in range(sub, sub + 1) if slot < SUBS + 2 * LAG else range(sub, SUBS):
            if sub >= 0:
                hops["1"][sub].wait_recv()
        sub = slot - 2 * LAG
        if 0 <= sub < SUBS:
            stage_1[sub] = jnp.where(
                m_part == 2, own[sub],
                jnp.where(m_part == 3, got_z[sub], jnp.where(m_part == 4, got_x[sub], got_z[sub + LAG])),
            )
            send_hop("1", stage_1.at[sub], got_1.at[sub])

    column_sum = jnp.zeros((8, COLS), F32)
    for k in range(CHUNKS):
        loads[k].wait()
        signed = rows[k] * sign[:, :, k % 2, k // 2]
        rows[k] = signed
        column_sum = column_sum + jnp.sum(signed.reshape(16, 8, COLS), axis=0)
        flat = signed.reshape(128, COLS)
        own[pl.ds(8 * k, 8)] = jnp.where(side128, flat[:, :HALF], flat[:, HALF:]).reshape(8, 16, HALF)
    sums[0] = jnp.sum(column_sum, axis=0, keepdims=True)
    with scope("bar"):
        pl.semaphore_wait(barrier, len(peers))
    sum_copies = []
    for mask in range(1, 8):
        sum_copies += start([(None, sums.at[0], sums.at[mask])], samp_peer(mask), fresh())

    natural = lax.broadcasted_iota(jnp.int32, (1, SG), 1)
    plans = [
        natural,
        jnp.where(seven_first, within[0:1], within[1:2]),
        jnp.where(seven_first, within[1:2], within[0:1]),
    ]

    def place_picks(index):
        plan = plans[index]
        p = plan >> 4
        place = ((plan >> 3) & 1) * 256 + (p & 1) * 128 + (p >> 3) * 32 + ((p >> 1) & 3) * 8 + (plan & 7)
        for first in range(0, SG, 128):
            position = lax.broadcasted_iota(jnp.int32, (128, SG), 0) + first
            picks[index, pl.ds(first, 128)] = jnp.where(position == place, 1.0, 0.0).astype(BF16)

    def centre():
        for _, copy in sum_copies:
            copy.wait_recv()
        mean = (
            ((sums[0] + sums[1]) + (sums[2] + sums[3])) + ((sums[4] + sums[5]) + (sums[6] + sums[7]))
        ) * (1.0 / SAMPLES)
        mean_ref[...] = jnp.where(side == 1, mean[:, HALF:], mean[:, :HALF])
        for k in range(CHUNKS):
            at = pl.ds(k * 128, 128)
            centred = rows[k].reshape(128, COLS) - mean
            c_high[at], c_low[at] = split(centred)
            h_high[at], h_low[at] = split(jnp.where(side128, centred[:, HALF:], centred[:, :HALF]))

    order_of = ((0, 3, 1, 2), (0, 1, 2, 3))
    hop_pairs = ((1, 3), (3, 1))

    def pair_of(index, q):
        low, high = bit_of(index, 0), bit_of(index, 1)
        return lax.rem(low + high, jnp.int32(2)) if q == 0 else high

    def place_in(index, q):
        return bit_of(index, 1 - q)

    def diagonal(c, half):
        rows_at, at = pl.ds(c * 256, 256), pl.ds(half * 256, 256)
        tile = product((c_high[rows_at], c_low[rows_at]), (c_high[at], c_low[at])).reshape(2, 4, 4, 8, 256)
        for i, to_y in enumerate(order_of[c]):
            for j, to_zh in enumerate(order_of[c]):
                pay_d[:, c, i, j, :, at] = tile[:, to_y, to_zh]

    def gather(k, kind):
        for j in range(8):
            sub = 8 * k + j
            if kind == 0:
                part_rows = jnp.where(z_first, got_x[sub + LAG], got_z[sub + LAG])
            else:
                part_rows = jnp.where(m_part == 1, got_z[sub], jnp.where(m_part == 6, got_x[sub], got_1[sub]))
            at = pl.ds(kind * 128 + 16 * j, 16)
            b_high[at], b_low[at] = split(part_rows - mean_ref[...])

    def tiles(k, kinds):
        at = pl.ds(kinds[0] * 128, len(kinds) * 128)
        tile = product((h_high[...], h_low[...]), (b_high[at], b_low[at]))
        own_tile = tile.reshape(2, 2, 4, 4, 8, len(kinds) * 128)
        back_tile = jnp.transpose(tile).reshape(len(kinds), 4, 4, 8, SG)
        for index, q in enumerate(kinds):
            lanes = slice(index * 128, index * 128 + 128)
            for i, to_y in enumerate(order_of[q]):
                for j, to_zh in enumerate(order_of[q]):
                    pay_b[k, q, i, j] = back_tile[index, to_y, to_zh]
                    for c in range(2):
                        pay_a[k, :, q, i, j, :, pl.ds(c * 128, 128)] = own_tile[c, :, to_y, to_zh, :, lanes]

    def halving(r0, r1, r2, r3, r4, wide, qs=(0, 1), ready=None):
        def hop(src, dst, peer):
            if wide is None:
                return start([(None, src, dst)], peer, fresh())
            first = pl.ds(0, 256)
            return start([(wide[0], src, dst), (wide[1], src.at[..., first], dst.at[..., first])], peer, fresh())

        def arrive(copies):
            for gate, copy in copies:
                if gate is None:
                    copy.wait_recv()
                else:
                    pl.when(gate)(copy.wait_recv)

        def add(dst, at, other):
            if wide is None:
                dst[at] = dst[at] + other[...]
                return
            first, rest = pl.ds(0, 256), pl.ds(256, SG)
            dst[at + (Ellipsis, first)] = dst[at + (Ellipsis, first)] + other[..., first]

            @pl.when(wide[0])
            def _():
                dst[at + (Ellipsis, rest)] = dst[at + (Ellipsis, rest)] + other[..., rest]

        steps = {}
        for q in qs:
            near = hop_pairs[q][0]
            peer = par_peer(flip(y, near, 2), zh, core)
            steps[q] = hop(r0.at[q, pl.ds(2 * (1 - pair_of(y, q)), 2)], r1.at[q], peer)
        yield
        nexts = {}
        for q in qs:
            far = hop_pairs[q][1]
            pair, place = pair_of(y, q), place_in(y, q)
            arrive(steps[q])
            add(r1, (q, 1 - place), r0.at[q, 2 * pair + 1 - place])
            nexts[q] = hop(r1.at[q, 1 - place], r2.at[q], par_peer(flip(y, far, 2), zh, core))
        for q in qs:
            pair, place = pair_of(y, q), place_in(y, q)
            add(r1, (q, place), r0.at[q, 2 * pair + place])
        yield
        steps = {}
        for q in qs:
            near = hop_pairs[q][0]
            arrive(nexts[q])
            add(r2, (q,), r1.at[q, place_in(y, q)])
            peer = par_peer(y, flip(zh, near, 2), core)
            steps[q] = hop(r2.at[q, pl.ds(2 * (1 - pair_of(zh, q)), 2)], r3.at[q], peer)
        yield
        nexts = {}
        for q in qs:
            far = hop_pairs[q][1]
            pair, place = pair_of(zh, q), place_in(zh, q)
            arrive(steps[q])
            add(r3, (q, 1 - place), r2.at[q, 2 * pair + 1 - place])
            nexts[q] = hop(r3.at[q, 1 - place], r4.at[q], par_peer(y, flip(zh, far, 2), core))
        for q in qs:
            pair, place = pair_of(zh, q), place_in(zh, q)
            add(r3, (q, place), r2.at[q, 2 * pair + place])
        yield
        for q in reversed(qs):
            arrive(nexts[q])
            add(r4, (q,), r3.at[q, place_in(zh, q)])
            if ready is not None:
                ready(q)

    def reduce_diagonal():
        ((_, step),) = start([(None, pay_d.at[1 - core], r0_d)], sibling, fresh())
        yield
        step.wait_recv()
        r0_d[...] = r0_d[...] + pay_d[core]
        yield from halving(r0_d, r1_d, r2_d, r3_d, r4_d, None)

    cross_sems = [[fresh() for _ in range(7)] for _ in range(2)]

    def reduce_chunk(k, kinds):
        c, to = k // 2, k % 2
        here, there = core == to, core != to
        first, rest = pl.ds(0, 256), pl.ds(256, SG)
        at = pl.ds(kinds[0], len(kinds))
        (_, step_a), (_, step_b) = start(
            [
                (here, pay_a.at[k, 1 - core, at], r0_c.at[k, at, ..., first]),
                (there, pay_b.at[k, at], r0_c.at[k, at, ..., rest]),
            ],
            sibling,
            fresh(),
        )
        yield

        @pl.when(there)
        def _():
            step_a.wait_recv()
            r0_c[k, at, ..., first] = r0_c[k, at, ..., first] + pay_a[k, 1 - to, at]

        @pl.when(here)
        def _():
            step_b.wait_recv()
            for q in kinds:
                places = [(order_of[q].index(to_y), order_of[q].index(to_zh)) for to_y in range(4) for to_zh in range(4)]
                for half in range(2):
                    lanes = pl.ds(256 + half * 256 + to * 128, 128)
                    block = jnp.concatenate([r0_c[k, q, i, j, :, lanes] for i, j in places], axis=0)
                    block = jnp.transpose(block).reshape(16, 8, 128)
                    lanes = pl.ds(half * 128, 128)
                    for place, (i, j) in enumerate(places):
                        r0_c[k, q, i, j, :, lanes] = pay_a[k, to, q, i, j, :, lanes] + block[place]
            r0_c[k, at, ..., rest] = r0_c[k, at, ..., rest] + pay_b[k, at]

        crossings = []

        def cross_over(kind):
            for mask in (7,) if kind == 0 else (5, 4, 3, 6, 2, 1):
                to_ref = cross_7.at[c] if kind == 0 else cross_m.at[c, mask - 1]
                ((_, copy),) = start(
                    [(here, r4_c.at[k, kind, :, rest], to_ref)], samp_peer(mask), cross_sems[c][mask - 1]
                )
                crossings.append(copy)

        yield from halving(
            r0_c.at[k], r1_c.at[k], r2_c.at[k], r3_c.at[k], r4_c.at[k], (here, there), kinds, cross_over
        )
        yield

        @pl.when(here)
        def _():
            for copy in crossings:
                copy.wait_recv()

    def ordered(value, index):
        value = value * (1.0 / SAMPLES)
        high, low = split(value)
        rest = value - high.astype(F32) - low.astype(F32)
        stacked = jnp.concatenate([high, low, rest.astype(BF16)], axis=0)
        moved = lax.dot_general(stacked, picks[index], (((1,), (0,)), ((), ())), preferred_element_type=F32)
        return moved[0:16] + (moved[16:32] + moved[32:48])

    def whole(kind):
        blocks = []
        for c in range(2):
            own_part = jnp.concatenate([r4_c[k, kind, :, pl.ds(c * 128, 128)] for k in range(CHUNKS)], axis=1)
            if kind == 0:
                arrived = cross_7[c]
            else:
                arrived = cross_m[c, 0]
                for mask in range(2, 7):
                    arrived = jnp.where(other == mask, cross_m[c, mask - 1], arrived)
            blocks.append(own_part + arrived)
        return jnp.concatenate(blocks, axis=0)

    walks = {}

    def advance(name):
        next(walks[name], None)

    def begin(name, walk):
        walks[name] = walk
        advance(name)

    def make_d(index):
        diagonal(index // 2, index % 2)
        if index == 3:
            begin("d", reduce_diagonal())

    both = (0, 1)

    def make(k, kinds):
        for kind in kinds:
            gather(k, kind)
        tiles(k, kinds)
        begin((k, kinds), reduce_chunk(k, kinds))

    c0, c1, c2, c3 = ((k, both) for k in range(4))
    after = {
        0: [(place_picks, 0)],
        1: [(place_picks, 1)],
        2: [(place_picks, 2)],
        7: [(centre,)],
        9: [(make_d, 0)],
        11: [(make_d, 1)],
        13: [(make_d, 2)],
        15: [(make_d, 3)],
        24: [(advance, "d")],
        26: [(make, 0, both)],
        31: [(advance, "d")],
        33: [(advance, c0)],
        34: [(make, 1, both)],
        40: [(advance, c0)],
        41: [(advance, c1)],
        42: [(make, 2, both), (advance, "d")],
        45: [(advance, c0), (advance, c2)],
        46: [(make, 3, both)],
    }
    for slot in range(SUBS + 2 * LAG + 1):
        with scope(f"ex{slot}"):
            exchange(slot)
        for job, *about in after.get(slot, []):
            with scope(f"job{slot}_{job.__name__}_{about}"):
                job(*about)
    def finish_d():
        tile_d = jnp.concatenate([r4_d[0], r4_d[1]], axis=0)
        out_ref[0, 0] = ordered(tile_d, 0)
        return tile_d
    for turn, name in enumerate((c1, c3, "d", c0, c2, c3, c1, "d", "tile", c2, c3, c0, c1, c2, c3, c1, c2, c3, c0, c1, c2, c3)):
        with scope(f"tail{turn}_{name}"):
            if name == "tile":
                tile_d = finish_d()
            else:
                advance(name)
    with scope("final"):
        tile_7 = ordered(whole(0), 1)
        tile_m = ordered(jnp.where(other == 0, tile_d, whole(1)), 2)
        out_ref[0, 1] = jnp.where(seven_first, tile_7, tile_m)
        out_ref[0, 2] = jnp.where(seven_first, tile_m, tile_7)
    with scope("drain"):
        for hop, copies in hops.items():
            for copy in copies[-len(hop_sems[hop]):]:
                copy.wait_send()
        for slot in range(SENDS):
            wait_sends(slot)


def gram(x, spins, roster):
    vmem = pltpu.VMEM

    def halves(lead, width):
        return [
            vmem(lead + (2, 4, 4, 8, width), F32),
            vmem(lead + (2, 2, 4, 8, width), F32),
            vmem(lead + (2, 4, 8, width), F32),
            vmem(lead + (2, 2, 8, width), F32),
            vmem(lead + (2, 8, width), F32),
        ]

    sets = [halves((), SG), halves((CHUNKS,), 256 + SG)]
    scratch = [
        vmem((CHUNKS, 4, 4, 8, COLS), F32),
        vmem((NSITES, SG), jnp.int32),
        vmem((2, SG), jnp.int32),
        vmem((SUBS, 16, HALF), F32),
        vmem((SLOTS, 16, HALF), F32),
        vmem((SLOTS, 16, HALF), F32),
        vmem((SUBS, 16, HALF), F32),
        vmem((SLOTS, 16, HALF), F32),
        vmem((SLOTS, 16, HALF), F32),
        vmem((SUBS, 16, HALF), F32),
        vmem((8, 1, COLS), F32),
        vmem((1, HALF), F32),
        vmem((SG, COLS), BF16),
        vmem((SG, COLS), BF16),
        vmem((SG, HALF), BF16),
        vmem((SG, HALF), BF16),
        vmem((256, HALF), BF16),
        vmem((256, HALF), BF16),
        vmem((2, 2, 4, 4, 8, SG), F32),
        vmem((CHUNKS, 2, 2, 4, 4, 8, 256), F32),
        vmem((CHUNKS, 2, 4, 4, 8, SG), F32),
        *[one[step] for step in range(5) for one in sets],
        vmem((2, 8, SG), F32),
        vmem((2, 6, 8, SG), F32),
        vmem((3, SG, SG), BF16),
        pltpu.SemaphoreType.DMA((6,)),
        pltpu.SemaphoreType.DMA((SENDS + 4 * LAG + 2 * LAST,)),
        pltpu.SemaphoreType.DMA((104,)),
    ]
    return pl.pallas_call(
        kernel,
        out_shape=jax.ShapeDtypeStruct((1, 3, 16, SG), F32),
        in_specs=[pl.BlockSpec(memory_space=pltpu.HBM)] * 3,
        out_specs=pl.BlockSpec(memory_space=pltpu.VMEM),
        scratch_shapes=scratch,
        compiler_params=pltpu.CompilerParams(
            collective_id=0, has_side_effects=True, vmem_limit_bytes=55040 * 1024
        ),
        name="gram",
    )(x, spins, roster)


def on_device(log_derivs, spins, roster):
    return gram(log_derivs.reshape(4, 4, 2, 2, 8, COLS), spins.T, roster)


def solution(mesh):
    in_specs = (P("samp", "par"), P("samp", None), P())
    out_specs = P("samp", None, "par", None)
    return jax.shard_map(
        on_device, mesh=mesh, in_specs=in_specs, out_specs=out_specs, check_vma=False
    )
```

```python
import functools

import jax
import jax.numpy as jnp
from jax import lax
from jax.experimental import pallas as pl
from jax.experimental.pallas import tpu as pltpu
from jax.sharding import PartitionSpec as P

MESH = pl.DeviceIdType.MESH
F32, BF16 = jnp.float32, jnp.bfloat16

SG = 512
NSITES = 100
LSIDE = 10
COLS = 1024
HALF = COLS // 2
SAMPLES = 4096
SUBS = 32
LAG = 7
SLOTS = SUBS + LAG
SENDS = 24
LAST = 5
CHUNKS = 4


def bit_of(value, index):
    return lax.rem(lax.div(value, jnp.int32(2**index)), jnp.int32(2))


def flip(value, mask, bits):
    total = jnp.int32(0)
    for index in range(bits):
        bit = bit_of(value, index)
        total = total + (1 - bit if mask >> index & 1 else bit) * 2**index
    return total


def dot_nt(left, right):
    return lax.dot_general(left, right, (((1,), (1,)), ((), ())), preferred_element_type=F32)


def split(value):
    high = value.astype(BF16)
    return high, (value - high.astype(F32)).astype(BF16)


def product(left, right):
    (left_high, left_low), (right_high, right_low) = left, right
    return dot_nt(left_high, right_high) + (dot_nt(left_high, right_low) + dot_nt(left_low, right_high))


def kernel(x_hbm, spins_hbm, roster_hbm, out_ref, *scratch):
    (rows, spins_ref, roster_ref, own, stage_x, stage_z, stage_1, got_x, got_z, got_1, sums, mean_ref,
     c_high, c_low, h_high, h_low, b_high, b_low, pay_d, pay_a, pay_b, r0_d, r0_c, r1_d, r1_c,
     r2_d, r2_c, r3_d, r3_c, r4_d, r4_c, cross_7, cross_m, picks,
     load_sem, send_sem, recv_sem) = scratch
    group = lax.axis_index("samp")
    part = lax.axis_index("par")
    core = lax.rem(part, jnp.int32(2))
    zh = lax.rem(lax.div(part, jnp.int32(2)), jnp.int32(4))
    y = lax.div(part, jnp.int32(8))

    def samp_peer(mask):
        return {"samp": flip(group, mask, 3)}

    def par_peer(new_y, new_zh, new_core):
        return {"par": new_y * 8 + new_zh * 2 + new_core}

    sibling = par_peer(y, zh, 1 - core)
    load_spins = pltpu.make_async_copy(spins_hbm, spins_ref, load_sem.at[4])
    load_roster = pltpu.make_async_copy(roster_hbm, roster_ref, load_sem.at[5])
    loads = [
        pltpu.make_async_copy(x_hbm.at[:, :, k % 2, k // 2], rows.at[k], load_sem.at[k]) for k in range(CHUNKS)
    ]
    for load in (load_roster, load_spins, *loads):
        load.start()

    peers = [samp_peer(mask) for mask in range(7, 0, -1)]
    peers += [par_peer(y, flip(zh, mask, 2), core) for mask in (1, 3)]
    peers += [par_peer(flip(y, mask, 2), zh, core) for mask in (1, 3)]
    peers += [sibling]
    barrier = pltpu.get_barrier_semaphore()
    for peer in peers:
        pl.semaphore_signal(barrier, inc=1, device_id=peer, device_id_type=MESH)

    def scope(name):
        return jax.named_scope(name)

    counter = [0]
    turn_of_send = [0]
    open_sends = [[] for _ in range(SENDS)]

    def fresh():
        counter[0] += 1
        return counter[0] - 1

    def remote(src, dst, peer, index, send_index):
        return pltpu.make_async_remote_copy(
            src_ref=src, dst_ref=dst, send_sem=send_sem.at[send_index], recv_sem=recv_sem.at[index],
            device_id=peer, device_id_type=MESH,
        )

    def wait_sends(slot):
        for gate, copy in open_sends[slot]:
            if gate is None:
                copy.wait_send()
            else:
                pl.when(gate)(copy.wait_send)
        open_sends[slot] = []

    def start(choices, peer, index):
        slot = turn_of_send[0] % SENDS
        turn_of_send[0] += 1
        wait_sends(slot)
        copies = []
        for gate, src, dst in choices:
            copy = remote(src, dst, peer, index, slot)
            if gate is None:
                copy.start()
            else:
                pl.when(gate)(copy.start)
            copies.append((gate, copy))
        open_sends[slot] = copies
        return copies

    load_roster.wait()
    masks = lax.shift_right_logical(roster_ref[...], 9)
    within = roster_ref[...] & (SG - 1)
    seven_first = masks[0:1] == 7
    other = jnp.where(seven_first, masks[1:2], masks[0:1])
    bits = [bit_of(group, index) for index in range(3)]
    side = jnp.where(other == 4, bits[2], jnp.where((other == 2) | (other == 6), bits[1], bits[0]))
    m_part = jnp.broadcast_to(other, (16, SG))
    z_first = (m_part == 1) | (m_part == 3)

    load_spins.wait()
    site = lax.broadcasted_iota(jnp.int32, (NSITES, SG), 0)
    on_a = lax.rem(lax.div(site, jnp.int32(LSIDE)) + lax.rem(site, jnp.int32(LSIDE)), jnp.int32(2)) == 0
    count = jnp.sum(jnp.where(on_a, spins_ref[...], 0).astype(F32), axis=0, keepdims=True)
    sign_row = 1.0 - 2.0 * (count - 2.0 * jnp.floor(count * 0.5))
    sign = jnp.transpose(jnp.broadcast_to(sign_row, (128, SG)))[:, 0:1].reshape(4, 4, 2, 2, 8, 1)
    side128 = jnp.broadcast_to(side, (128, SG)) == 1
    hops = {"x": [], "z": [], "1": []}
    hop_masks = {"x": 6, "z": 1, "1": 2}
    hop_sems = {hop: [fresh() for _ in range(2 * (LAST if hop == "1" else LAG))] for hop in hops}
    hop_sends = {hop: [SENDS + index for index in sems] for hop, sems in hop_sems.items()}

    def send_hop(hop, src, dst):
        sems, copies = hop_sems[hop], hops[hop]
        if len(copies) >= len(sems):
            copies[-len(sems)].wait_send()
        turn = len(copies) % len(sems)
        copy = remote(src, dst, samp_peer(hop_masks[hop]), sems[turn], hop_sends[hop][turn])
        copy.start()
        copies.append(copy)

    def exchange(slot):
        before = slot - LAG
        if 0 <= before < SLOTS:
            for hop in "xz":
                hops[hop][before].wait_recv()
        if slot < SLOTS:
            if slot < LAG:
                from_x = from_z = own.at[slot]
            elif slot < SUBS:
                stage_x[slot] = jnp.where(z_first, got_z[before], own[slot])
                stage_z[slot] = jnp.where(z_first, own[slot], got_x[before])
                from_x, from_z = stage_x.at[slot], stage_z.at[slot]
            else:
                from_x, from_z = got_z.at[before], got_x.at[before]
            send_hop("x", from_x, got_x.at[slot])
            send_hop("z", from_z, got_z.at[slot])
        sub = slot - 2 * LAG - LAST
        for sub in range(sub, sub + 1) if slot < SUBS + 2 * LAG else range(sub, SUBS):
            if sub >= 0:
                hops["1"][sub].wait_recv()
        sub = slot - 2 * LAG
        if 0 <= sub < SUBS:
            stage_1[sub] = jnp.where(
                m_part == 2, own[sub],
                jnp.where(m_part == 3, got_z[sub], jnp.where(m_part == 4, got_x[sub], got_z[sub + LAG])),
            )
            send_hop("1", stage_1.at[sub], got_1.at[sub])

    column_sum = jnp.zeros((8, COLS), F32)
    for k in range(CHUNKS):
        loads[k].wait()
        signed = rows[k] * sign[:, :, k % 2, k // 2]
        rows[k] = signed
        column_sum = column_sum + jnp.sum(signed.reshape(16, 8, COLS), axis=0)
        flat = signed.reshape(128, COLS)
        own[pl.ds(8 * k, 8)] = jnp.where(side128, flat[:, :HALF], flat[:, HALF:]).reshape(8, 16, HALF)
    sums[0] = jnp.sum(column_sum, axis=0, keepdims=True)
    with scope("bar"):
        pl.semaphore_wait(barrier, len(peers))
    sum_copies = []
    for mask in range(1, 8):
        sum_copies += start([(None, sums.at[0], sums.at[mask])], samp_peer(mask), fresh())

    natural = lax.broadcasted_iota(jnp.int32, (1, SG), 1)
    plans = [
        natural,
        jnp.where(seven_first, within[0:1], within[1:2]),
        jnp.where(seven_first, within[1:2], within[0:1]),
    ]

    def place_picks(index):
        plan = plans[index]
        p = plan >> 4
        place = ((plan >> 3) & 1) * 256 + (p & 1) * 128 + (p >> 3) * 32 + ((p >> 1) & 3) * 8 + (plan & 7)
        for first in range(0, SG, 128):
            position = lax.broadcasted_iota(jnp.int32, (128, SG), 0) + first
            picks[index, pl.ds(first, 128)] = jnp.where(position == place, 1.0, 0.0).astype(BF16)

    def centre():
        for _, copy in sum_copies:
            copy.wait_recv()
        mean = (
            ((sums[0] + sums[1]) + (sums[2] + sums[3])) + ((sums[4] + sums[5]) + (sums[6] + sums[7]))
        ) * (1.0 / SAMPLES)
        mean_ref[...] = jnp.where(side == 1, mean[:, HALF:], mean[:, :HALF])
        for k in range(CHUNKS):
            at = pl.ds(k * 128, 128)
            centred = rows[k].reshape(128, COLS) - mean
            c_high[at], c_low[at] = split(centred)
            h_high[at], h_low[at] = split(jnp.where(side128, centred[:, HALF:], centred[:, :HALF]))

    order_of = ((0, 3, 1, 2), (0, 1, 2, 3))
    hop_pairs = ((1, 3), (3, 1))

    def pair_of(index, q):
        low, high = bit_of(index, 0), bit_of(index, 1)
        return lax.rem(low + high, jnp.int32(2)) if q == 0 else high

    def place_in(index, q):
        return bit_of(index, 1 - q)

    def diagonal(c, half):
        rows_at, at = pl.ds(c * 256, 256), pl.ds(half * 256, 256)
        tile = product((c_high[rows_at], c_low[rows_at]), (c_high[at], c_low[at])).reshape(2, 4, 4, 8, 256)
        for i, to_y in enumerate(order_of[c]):
            for j, to_zh in enumerate(order_of[c]):
                pay_d[:, c, i, j, :, at] = tile[:, to_y, to_zh]

    def gather(k, kind):
        for j in range(8):
            sub = 8 * k + j
            if kind == 0:
                part_rows = jnp.where(z_first, got_x[sub + LAG], got_z[sub + LAG])
            else:
                part_rows = jnp.where(m_part == 1, got_z[sub], jnp.where(m_part == 6, got_x[sub], got_1[sub]))
            at = pl.ds(kind * 128 + 16 * j, 16)
            b_high[at], b_low[at] = split(part_rows - mean_ref[...])

    def tiles(k, kinds):
        at = pl.ds(kinds[0] * 128, len(kinds) * 128)
        tile = product((h_high[...], h_low[...]), (b_high[at], b_low[at]))
        own_tile = tile.reshape(2, 2, 4, 4, 8, len(kinds) * 128)
        back_tile = jnp.transpose(tile).reshape(len(kinds), 4, 4, 8, SG)
        for index, q in enumerate(kinds):
            lanes = slice(index * 128, index * 128 + 128)
            for i, to_y in enumerate(order_of[q]):
                for j, to_zh in enumerate(order_of[q]):
                    pay_b[k, q, i, j] = back_tile[index, to_y, to_zh]
                    for c in range(2):
                        pay_a[k, :, q, i, j, :, pl.ds(c * 128, 128)] = own_tile[c, :, to_y, to_zh, :, lanes]

    def halving(r0, r1, r2, r3, r4, wide, qs=(0, 1), ready=None):
        def hop(src, dst, peer):
            if wide is None:
                return start([(None, src, dst)], peer, fresh())
            first = pl.ds(0, 256)
            return start([(wide[0], src, dst), (wide[1], src.at[..., first], dst.at[..., first])], peer, fresh())

        def arrive(copies):
            for gate, copy in copies:
                if gate is None:
                    copy.wait_recv()
                else:
                    pl.when(gate)(copy.wait_recv)

        def add(dst, at, other):
            if wide is None:
                dst[at] = dst[at] + other[...]
                return
            first, rest = pl.ds(0, 256), pl.ds(256, SG)
            dst[at + (Ellipsis, first)] = dst[at + (Ellipsis, first)] + other[..., first]

            @pl.when(wide[0])
            def _():
                dst[at + (Ellipsis, rest)] = dst[at + (Ellipsis, rest)] + other[..., rest]

        steps = {}
        for q in qs:
            near = hop_pairs[q][0]
            peer = par_peer(flip(y, near, 2), zh, core)
            steps[q] = hop(r0.at[q, pl.ds(2 * (1 - pair_of(y, q)), 2)], r1.at[q], peer)
        yield
        nexts = {}
        for q in qs:
            far = hop_pairs[q][1]
            pair, place = pair_of(y, q), place_in(y, q)
            arrive(steps[q])
            add(r1, (q, 1 - place), r0.at[q, 2 * pair + 1 - place])
            nexts[q] = hop(r1.at[q, 1 - place], r2.at[q], par_peer(flip(y, far, 2), zh, core))
        for q in qs:
            pair, place = pair_of(y, q), place_in(y, q)
            add(r1, (q, place), r0.at[q, 2 * pair + place])
        yield
        steps = {}
        for q in qs:
            near = hop_pairs[q][0]
            arrive(nexts[q])
            add(r2, (q,), r1.at[q, place_in(y, q)])
            peer = par_peer(y, flip(zh, near, 2), core)
            steps[q] = hop(r2.at[q, pl.ds(2 * (1 - pair_of(zh, q)), 2)], r3.at[q], peer)
        yield
        nexts = {}
        for q in qs:
            far = hop_pairs[q][1]
            pair, place = pair_of(zh, q), place_in(zh, q)
            arrive(steps[q])
            add(r3, (q, 1 - place), r2.at[q, 2 * pair + 1 - place])
            nexts[q] = hop(r3.at[q, 1 - place], r4.at[q], par_peer(y, flip(zh, far, 2), core))
        for q in qs:
            pair, place = pair_of(zh, q), place_in(zh, q)
            add(r3, (q, place), r2.at[q, 2 * pair + place])
        yield
        for q in reversed(qs):
            arrive(nexts[q])
            add(r4, (q,), r3.at[q, place_in(zh, q)])
            if ready is not None:
                ready(q)

    def reduce_diagonal():
        ((_, step),) = start([(None, pay_d.at[1 - core], r0_d)], sibling, fresh())
        yield
        step.wait_recv()
        r0_d[...] = r0_d[...] + pay_d[core]
        yield from halving(r0_d, r1_d, r2_d, r3_d, r4_d, None)

    cross_sems = [[fresh() for _ in range(7)] for _ in range(2)]

    def reduce_chunk(k, kinds):
        c, to = k // 2, k % 2
        here, there = core == to, core != to
        first, rest = pl.ds(0, 256), pl.ds(256, SG)
        at = pl.ds(kinds[0], len(kinds))
        (_, step_a), (_, step_b) = start(
            [
                (here, pay_a.at[k, 1 - core, at], r0_c.at[k, at, ..., first]),
                (there, pay_b.at[k, at], r0_c.at[k, at, ..., rest]),
            ],
            sibling,
            fresh(),
        )
        yield

        @pl.when(there)
        def _():
            step_a.wait_recv()
            r0_c[k, at, ..., first] = r0_c[k, at, ..., first] + pay_a[k, 1 - to, at]

        @pl.when(here)
        def _():
            step_b.wait_recv()
            for q in kinds:
                places = [(order_of[q].index(to_y), order_of[q].index(to_zh)) for to_y in range(4) for to_zh in range(4)]
                for half in range(2):
                    lanes = pl.ds(256 + half * 256 + to * 128, 128)
                    block = jnp.concatenate([r0_c[k, q, i, j, :, lanes] for i, j in places], axis=0)
                    block = jnp.transpose(block).reshape(16, 8, 128)
                    lanes = pl.ds(half * 128, 128)
                    for place, (i, j) in enumerate(places):
                        r0_c[k, q, i, j, :, lanes] = pay_a[k, to, q, i, j, :, lanes] + block[place]
            r0_c[k, at, ..., rest] = r0_c[k, at, ..., rest] + pay_b[k, at]

        crossings = []

        def cross_over(kind):
            for mask in (7,) if kind == 0 else (5, 4, 3, 6, 2, 1):
                to_ref = cross_7.at[c] if kind == 0 else cross_m.at[c, mask - 1]
                ((_, copy),) = start(
                    [(here, r4_c.at[k, kind, :, rest], to_ref)], samp_peer(mask), cross_sems[c][mask - 1]
                )
                crossings.append(copy)

        yield from halving(
            r0_c.at[k], r1_c.at[k], r2_c.at[k], r3_c.at[k], r4_c.at[k], (here, there), kinds, cross_over
        )
        yield

        @pl.when(here)
        def _():
            for copy in crossings:
                copy.wait_recv()

    def ordered(value, index):
        value = value * (1.0 / SAMPLES)
        high, low = split(value)
        rest = value - high.astype(F32) - low.astype(F32)
        stacked = jnp.concatenate([high, low, rest.astype(BF16)], axis=0)
        moved = lax.dot_general(stacked, picks[index], (((1,), (0,)), ((), ())), preferred_element_type=F32)
        return moved[0:16] + (moved[16:32] + moved[32:48])

    def whole(kind):
        blocks = []
        for c in range(2):
            own_part = jnp.concatenate([r4_c[k, kind, :, pl.ds(c * 128, 128)] for k in range(CHUNKS)], axis=1)
            if kind == 0:
                arrived = cross_7[c]
            else:
                arrived = cross_m[c, 0]
                for mask in range(2, 7):
                    arrived = jnp.where(other == mask, cross_m[c, mask - 1], arrived)
            blocks.append(own_part + arrived)
        return jnp.concatenate(blocks, axis=0)

    walks = {}

    def advance(name):
        next(walks[name], None)

    def begin(name, walk):
        walks[name] = walk
        advance(name)

    def make_d(index):
        diagonal(index // 2, index % 2)
        if index == 3:
            begin("d", reduce_diagonal())

    both = (0, 1)

    def make(k, kinds):
        for kind in kinds:
            gather(k, kind)
        tiles(k, kinds)
        begin((k, kinds), reduce_chunk(k, kinds))

    c0, c1, c2, c3 = ((k, both) for k in range(4))
    after = {
        0: [(place_picks, 0)],
        1: [(place_picks, 1)],
        2: [(place_picks, 2)],
        7: [(centre,)],
        9: [(make_d, 0)],
        11: [(make_d, 1)],
        13: [(make_d, 2)],
        15: [(make_d, 3)],
        24: [(advance, "d")],
        26: [(make, 0, both)],
        31: [(advance, "d")],
        33: [(advance, c0)],
        34: [(make, 1, both)],
        40: [(advance, c0)],
        41: [(advance, c1)],
        42: [(make, 2, both), (advance, "d")],
        45: [(advance, c0), (advance, c2)],
        46: [(make, 3, both)],
    }
    for slot in range(SUBS + 2 * LAG + 1):
        with scope(f"ex{slot}"):
            exchange(slot)
        for job, *about in after.get(slot, []):
            with scope(f"job{slot}_{job.__name__}_{about}"):
                job(*about)
    def finish_d():
        tile_d = jnp.concatenate([r4_d[0], r4_d[1]], axis=0)
        out_ref[0, 0] = ordered(tile_d, 0)
        return tile_d
    for turn, name in enumerate((c1, c3, "d", c0, c2, c3, c1, "d", c2, c3, c1, c2, c3, "tile", c0, c1, c2, c3, c0, c1, c2, c3)):
        with scope(f"tail{turn}_{name}"):
            if name == "tile":
                tile_d = finish_d()
            else:
                advance(name)
    with scope("final"):
        tile_7 = ordered(whole(0), 1)
        tile_m = ordered(jnp.where(other == 0, tile_d, whole(1)), 2)
        out_ref[0, 1] = jnp.where(seven_first, tile_7, tile_m)
        out_ref[0, 2] = jnp.where(seven_first, tile_m, tile_7)
    with scope("drain"):
        for hop, copies in hops.items():
            for copy in copies[-len(hop_sems[hop]):]:
                copy.wait_send()
        for slot in range(SENDS):
            wait_sends(slot)


def gram(x, spins, roster):
    vmem = pltpu.VMEM

    def halves(lead, width):
        return [
            vmem(lead + (2, 4, 4, 8, width), F32),
            vmem(lead + (2, 2, 4, 8, width), F32),
            vmem(lead + (2, 4, 8, width), F32),
            vmem(lead + (2, 2, 8, width), F32),
            vmem(lead + (2, 8, width), F32),
        ]

    sets = [halves((), SG), halves((CHUNKS,), 256 + SG)]
    scratch = [
        vmem((CHUNKS, 4, 4, 8, COLS), F32),
        vmem((NSITES, SG), jnp.int32),
        vmem((2, SG), jnp.int32),
        vmem((SUBS, 16, HALF), F32),
        vmem((SLOTS, 16, HALF), F32),
        vmem((SLOTS, 16, HALF), F32),
        vmem((SUBS, 16, HALF), F32),
        vmem((SLOTS, 16, HALF), F32),
        vmem((SLOTS, 16, HALF), F32),
        vmem((SUBS, 16, HALF), F32),
        vmem((8, 1, COLS), F32),
        vmem((1, HALF), F32),
        vmem((SG, COLS), BF16),
        vmem((SG, COLS), BF16),
        vmem((SG, HALF), BF16),
        vmem((SG, HALF), BF16),
        vmem((256, HALF), BF16),
        vmem((256, HALF), BF16),
        vmem((2, 2, 4, 4, 8, SG), F32),
        vmem((CHUNKS, 2, 2, 4, 4, 8, 256), F32),
        vmem((CHUNKS, 2, 4, 4, 8, SG), F32),
        *[one[step] for step in range(5) for one in sets],
        vmem((2, 8, SG), F32),
        vmem((2, 6, 8, SG), F32),
        vmem((3, SG, SG), BF16),
        pltpu.SemaphoreType.DMA((6,)),
        pltpu.SemaphoreType.DMA((SENDS + 4 * LAG + 2 * LAST,)),
        pltpu.SemaphoreType.DMA((104,)),
    ]
    return pl.pallas_call(
        kernel,
        out_shape=jax.ShapeDtypeStruct((1, 3, 16, SG), F32),
        in_specs=[pl.BlockSpec(memory_space=pltpu.HBM)] * 3,
        out_specs=pl.BlockSpec(memory_space=pltpu.VMEM),
        scratch_shapes=scratch,
        compiler_params=pltpu.CompilerParams(
            collective_id=0, has_side_effects=True, vmem_limit_bytes=55040 * 1024
        ),
        name="gram",
    )(x, spins, roster)


def on_device(log_derivs, spins, roster):
    return gram(log_derivs.reshape(4, 4, 2, 2, 8, COLS), spins.T, roster)


def solution(mesh):
    in_specs = (P("samp", "par"), P("samp", None), P())
    out_specs = P("samp", None, "par", None)
    return jax.shard_map(
        on_device, mesh=mesh, in_specs=in_specs, out_specs=out_specs, check_vma=False
    )
```
